512 devices in a mesh: replica: 64 (over y_hi, z, core), tp: 8 (over y_lo, x).
Axes of the slice: x: 4, y: 8 (y_hi: 4, y_lo: 2; y = y_hi * 2 + y_lo), z: 8, core: 2. Of those that a mesh axis runs over, the one named last changes fastest.
Arguments:
- queries: bfloat16 [256, 32, 128], P('replica', 'tp'), may hold values from -14 to 14
- key_new: bfloat16 [256, 8, 128], P('replica', 'tp'), may hold values from -7.2 to 7.2
- new_token_value: bfloat16 [256, 8, 128], P('replica', 'tp'), may hold values from -6 to 6
- key_pool: bfloat16 [512, 8, 128, 128], P('replica', 'tp'), may hold values from -4 to 4
- value_block_pool: bfloat16 [512, 8, 128, 128], P('replica', 'tp'), may hold values from -6 to 6
- block_table: int32 [256, 2], P('replica'), may hold values from 0 to 7, as said below
- cache_blocks: int32 [256], P('replica'), may hold values from 1 to 2, as said below
- mig_request: int32 [128], P('replica'), may hold values from 0 to 3, as said below
- mig_dest: int32 [128], P('replica'), may hold values from 0 to 63, as said below
- levels: bfloat16 [4096, 4096], P('tp'), may hold values from -127 to 127, as said below
- chan_scale: float32 [4096], P('tp'), may hold values from 0.001 to 0.01
- residual: bfloat16 [256, 4096], P('replica', 'tp'), may hold values from -24 to 24
- norm_gain: float32 [4096], P('tp'), may hold values from 0.5 to 1.5
Outputs:
- hidden: bfloat16 [256, 4096], P('replica', 'tp')
- normed: bfloat16 [256, 4096], P('replica', 'tp')
- recv_key: bfloat16 [128, 2, 8, 128, 128], P('replica', None, 'tp')
- recv_value: bfloat16 [128, 2, 8, 128, 128], P('replica', None, 'tp')
- recv_count: int32 [128], P('replica')
- recv_source: int32 [128], P('replica')
The draws below stay inside these ranges and needn't reach their ends.
Inputs may be any that keep to these rules, and one draw needn't show every extreme that they name: `block_table`: the 4 x 2 entries of one replica name each of its 8 pool blocks once. `cache_blocks`: every replica has a request with 2 blocks. `mig_request`: the 2 entries of one replica name different requests; some replica lists a request with 2 blocks. `mig_dest`: for each j, entry j of the 64 replicas names every replica exactly once, and no replica names itself. `levels`: whole numbers.
All inputs are finite; a program needn't handle non-finite values.
Results may differ from the reference program's by a relative error of at most 0.024.
Values may be sent and summed in bfloat16 or wider, within the bound.
A program may use at most 128 MiB of HBM per device.

```python
import math
import jax
import jax.numpy as jnp
from jax import lax

DW = 4096
QUERY_HEADS = 32
KEY_VALUE_HEADS = 8
HEAD_SIZE = 128
BLOCK_TOKENS = 128
REQUEST_COUNT = 4
MAX_BLOCK_COUNT = 2
MIGS = 2
POOL_BLOCKS = 8
REPLICA_COUNT = 64


def shared_query_base(key):
    base_offset = jax.random.normal(jax.random.fold_in(key, 102), (REPLICA_COUNT * REQUEST_COUNT, QUERY_HEADS, HEAD_SIZE), jnp.float32)
    return jnp.clip(base_offset, -4.0, 4.0)


def migration_plan(key):
    first_part, second_part, third, fourth, fifth = jax.random.split(jax.random.fold_in(key, 200), 5)
    columns = jnp.arange(REQUEST_COUNT, dtype=jnp.int32)[None, :]
    lengths = jax.random.randint(first_part, (REPLICA_COUNT, REQUEST_COUNT), 1, MAX_BLOCK_COUNT + 1)
    longest = jax.random.randint(second_part, (REPLICA_COUNT, 1), 0, REQUEST_COUNT)
    lengths = jnp.where(columns == longest, MAX_BLOCK_COUNT, lengths)
    flags = jax.random.randint(third, (REPLICA_COUNT, 1), 0, 2)
    pivot = jax.random.randint(fourth, (), 0, REPLICA_COUNT)
    flags = jnp.maximum(flags, (jnp.arange(REPLICA_COUNT, dtype=jnp.int32)[:, None] == pivot).astype(jnp.int32))
    orders = jax.vmap(lambda k: jax.random.permutation(k, REQUEST_COUNT))(jax.random.split(fifth, REPLICA_COUNT))
    scores = orders.astype(jnp.int32) + flags * REQUEST_COUNT * (columns == longest).astype(jnp.int32)
    chosen = jnp.argsort(-scores, axis=1)[:, :MIGS]
    return (lengths.astype(jnp.int32), chosen.astype(jnp.int32))


def draw_queries(key, part):
    base_offset = shared_query_base(key)
    values = base_offset
    return values.astype(jnp.bfloat16)


def draw_key_new(key, part):
    base_offset = shared_query_base(key)
    key = jax.random.fold_in(key, 2)
    grouped_heads = jnp.mean(base_offset.reshape(REPLICA_COUNT * REQUEST_COUNT, KEY_VALUE_HEADS, QUERY_HEADS // KEY_VALUE_HEADS, HEAD_SIZE), axis=2)
    random_noise = jnp.clip(jax.random.normal(key, (REPLICA_COUNT * REQUEST_COUNT, KEY_VALUE_HEADS, HEAD_SIZE), jnp.float32), -4.0, 4.0)
    return (0.3 * random_noise + 1.5 * grouped_heads).astype(jnp.bfloat16)


def draw_key_pool(key, part):
    key = jax.random.fold_in(key, 3)
    first_part = jax.random.fold_in(key, 0)
    random_noise = jnp.clip(jax.random.normal(first_part, (REPLICA_COUNT * POOL_BLOCKS, KEY_VALUE_HEADS, BLOCK_TOKENS, HEAD_SIZE), jnp.float32), -4.0, 4.0)
    values = random_noise
    return values.astype(jnp.bfloat16)


def draw_block_table(key, part):
    key = jax.random.fold_in(key, 4)
    orders = jax.vmap(lambda k: jax.random.permutation(k, POOL_BLOCKS))(jax.random.split(key, REPLICA_COUNT))
    return orders.reshape(REPLICA_COUNT * REQUEST_COUNT, MAX_BLOCK_COUNT).astype(jnp.int32)


def draw_cache_blocks(key, part):
    lengths, chosen = migration_plan(key)
    return lengths.reshape(REPLICA_COUNT * REQUEST_COUNT)


def draw_mig_request(key, part):
    lengths, chosen = migration_plan(key)
    return chosen.reshape(REPLICA_COUNT * MIGS)


def one_derangement(key):
    first_part, second_part = jax.random.split(key)
    order = jax.random.permutation(first_part, REPLICA_COUNT).astype(jnp.int32)
    inverse = jnp.argsort(order).astype(jnp.int32)
    step = jax.random.randint(second_part, (), 1, REPLICA_COUNT)
    return order[(inverse + step) % REPLICA_COUNT].astype(jnp.int32)


def draw_mig_dest(key, part):
    key = jax.random.fold_in(key, 6)
    columns = jax.vmap(one_derangement)(jax.random.split(key, MIGS))
    return jnp.transpose(columns).reshape(REPLICA_COUNT * MIGS).astype(jnp.int32)


def draw_levels(key, part):
    key = jax.random.fold_in(key, 7)
    whole = jax.random.randint(key, (QUERY_HEADS * HEAD_SIZE, DW), -127, 128)
    return whole.astype(jnp.float32).astype(jnp.bfloat16)


def draw_residual(key, part):
    key = jax.random.fold_in(key, 8)
    first_part, second_part, third = jax.random.split(key, 3)
    row_scale = jnp.exp(jax.random.uniform(first_part, (REPLICA_COUNT * REQUEST_COUNT, 1), jnp.float32, math.log(0.3), math.log(3.0)))
    spot = jax.random.uniform(second_part, (DW,), jnp.float32, 0.0, 1.0)
    column_scale = jnp.power(10.0, 0.5 * jnp.arange(DW, dtype=jnp.float32) / DW + 0.5 * spot)
    base_offset = jnp.clip(jax.random.normal(third, (REPLICA_COUNT * REQUEST_COUNT, DW), jnp.float32), -4.0, 4.0)
    return (0.2 * base_offset * row_scale * column_scale[None, :]).astype(jnp.bfloat16)


def shard_levels(own_key, dims, shards, smallest, top_value):
    def one(position, blocks):
        heights = jax.random.uniform(jax.random.fold_in(jax.random.fold_in(own_key, 6), position), (blocks,), jnp.float32, smallest / len(shards), top_value / len(shards))
        return jnp.repeat(jnp.exp(heights), dims[position] // blocks).reshape((-1,) + (1,) * (len(dims) - position - 1))

    gain = one(*shards[0])
    for cut in shards[1:]:
        gain = gain * one(*cut)
    return gain


def scatter_about(own_key, dims, deviation, limit, cuts=(), kind=jnp.bfloat16):
    drawn = jax.random.normal(own_key, dims, jnp.float32) * deviation
    if len(cuts) > 0:
        drawn = shard_levels(own_key, dims, cuts, -0.22, 0.18) * drawn
    return jnp.clip(drawn, min=-limit, max=limit).astype(kind)


def setup_inputs(seed: int = 0) -> dict:
    streams_of = jax.random.split(jax.random.key(seed), 14)
    queries = draw_queries(jax.random.fold_in(streams_of[13], 71), 0)
    key_new = draw_key_new(jax.random.fold_in(streams_of[13], 71), 0)
    new_token_value = scatter_about(streams_of[2], (REPLICA_COUNT * REQUEST_COUNT, KEY_VALUE_HEADS, HEAD_SIZE), 1.0, 6.0, ((0, 64), (1, 8)))
    key_pool = draw_key_pool(jax.random.fold_in(streams_of[13], 71), 0)
    value_block_pool = scatter_about(streams_of[4], (REPLICA_COUNT * POOL_BLOCKS, KEY_VALUE_HEADS, BLOCK_TOKENS, HEAD_SIZE), 1.0, 6.0, ((0, 64), (1, 8)))
    block_table = draw_block_table(jax.random.fold_in(streams_of[13], 71), 0)
    cache_blocks = draw_cache_blocks(jax.random.fold_in(streams_of[13], 71), 0)
    mig_request = draw_mig_request(jax.random.fold_in(streams_of[13], 71), 0)
    mig_dest = draw_mig_dest(jax.random.fold_in(streams_of[13], 71), 0)
    levels = draw_levels(jax.random.fold_in(streams_of[13], 71), 0)
    chan_scale = jnp.clip(jnp.exp(math.log(0.01) - 2.30258502 * jax.random.uniform(streams_of[10], (DW,), jnp.float32) ** shard_levels(streams_of[10], (DW,), ((0, 8),), -0.2, 0.2)), 0.001, 0.01)
    residual = draw_residual(jax.random.fold_in(streams_of[13], 71), 0)
    norm_gain = jnp.clip(1.0 + 0.1 * jax.random.normal(streams_of[12], (DW,), jnp.float32), 0.5, 1.5)
    return {"queries": queries, "key_new": key_new, "new_token_value": new_token_value, "key_pool": key_pool, "value_block_pool": value_block_pool, "block_table": block_table, "cache_blocks": cache_blocks, "mig_request": mig_request, "mig_dest": mig_dest, "levels": levels, "chan_scale": chan_scale, "residual": residual, "norm_gain": norm_gain}


def attend(queries, key_new, new_token_value, keys, values, cache_blocks):
    request_rows, kv_heads, span, width = keys.shape
    grouped_heads = queries.reshape(request_rows, kv_heads, -1, width).astype(jnp.float32)
    scale = 1.0 / math.sqrt(width)
    scores = jnp.einsum('rkgd,rktd->rkgt', grouped_heads, keys.astype(jnp.float32)) * scale
    own = jnp.einsum('rkgd,rkd->rkg', grouped_heads, key_new.astype(jnp.float32)) * scale
    live = jnp.arange(span, dtype=jnp.int32)[None, :] < (cache_blocks * BLOCK_TOKENS)[:, None]
    live = live[:, None, None, :]
    masked = jnp.where(live, scores, jnp.float32(-1e+30))
    top = jnp.maximum(lax.optimization_barrier(jnp.max(masked, axis=-1)), own)
    expo = jnp.where(live, jnp.exp(masked - top[..., None]), jnp.float32(0.0))
    self_expo = jnp.exp(own - top)
    total = lax.optimization_barrier(jnp.sum(expo, axis=-1)) + self_expo
    weights = (expo / total[..., None]).astype(jnp.bfloat16)
    self_weight = (self_expo / total).astype(jnp.bfloat16)
    mixed = jnp.einsum('rkgt,rktd->rkgd', weights.astype(jnp.float32), values.astype(jnp.float32))
    mixed = mixed + self_weight.astype(jnp.float32)[..., None] * new_token_value.astype(jnp.float32)[:, :, None, :]
    return mixed.reshape(request_rows, -1).astype(jnp.bfloat16)

def reference(queries, key_new, new_token_value, key_pool, value_block_pool, block_table, cache_blocks, mig_request, mig_dest, levels, chan_scale, residual, norm_gain):
    request_rows = queries.shape[0]
    replica_of = jnp.arange(request_rows, dtype=jnp.int32) // REQUEST_COUNT
    global_block_table = (block_table + (replica_of * POOL_BLOCKS)[:, None]).astype(jnp.int32)

    def cached(block_pool):
        picked_blocks = jnp.take(block_pool, global_block_table.reshape(-1), axis=0).reshape(request_rows, MAX_BLOCK_COUNT, KEY_VALUE_HEADS, BLOCK_TOKENS, HEAD_SIZE)
        return jnp.transpose(picked_blocks, (0, 2, 1, 3, 4)).reshape(request_rows, KEY_VALUE_HEADS, MAX_BLOCK_COUNT * BLOCK_TOKENS, HEAD_SIZE)
    attn = attend(queries, key_new, new_token_value, cached(key_pool), cached(value_block_pool), cache_blocks)
    summed = jnp.dot(attn, levels, preferred_element_type=jnp.float32)
    hidden = (summed * chan_scale[None, :] + residual.astype(jnp.float32)).astype(jnp.bfloat16)
    wide = lax.optimization_barrier(hidden).astype(jnp.float32)
    mean_square = lax.optimization_barrier(jnp.mean(wide * wide, axis=-1))
    normed = (wide * lax.rsqrt(mean_square + 1e-05)[:, None] * norm_gain[None, :]).astype(jnp.bfloat16)
    table_entries = REPLICA_COUNT * MIGS
    source = jnp.arange(table_entries, dtype=jnp.int32) // MIGS
    request = (source * REQUEST_COUNT + mig_request).astype(jnp.int32)
    counts = cache_blocks[request]
    block_tables = (block_table[request] + (source * POOL_BLOCKS)[:, None]).astype(jnp.int32)
    live = jnp.arange(MAX_BLOCK_COUNT, dtype=jnp.int32)[None, :] < counts[:, None]

    def moved(block_pool):
        picked_blocks = jnp.take(block_pool, block_tables.reshape(-1), axis=0).reshape(table_entries, MAX_BLOCK_COUNT, KEY_VALUE_HEADS, BLOCK_TOKENS, HEAD_SIZE)
        return jnp.where(live[:, :, None, None, None], picked_blocks, jnp.zeros_like(picked_blocks))
    target = (mig_dest * MIGS + jnp.arange(table_entries, dtype=jnp.int32) % MIGS).astype(jnp.int32)
    moved_key = moved(key_pool)
    moved_value = moved(value_block_pool)
    recv_key = jnp.zeros_like(moved_key).at[target].set(moved_key)
    recv_value = jnp.zeros_like(moved_value).at[target].set(moved_value)
    recv_count = jnp.zeros((table_entries,), jnp.int32).at[target].set(counts)
    recv_source = jnp.zeros((table_entries,), jnp.int32).at[target].set(source)
    return (hidden, normed, recv_key, recv_value, recv_count, recv_source)
```

```python
import functools
import math

import jax
import jax.numpy as jnp
from jax import lax
from jax.experimental import pallas as pl
from jax.experimental.pallas import tpu as pltpu
from jax.sharding import PartitionSpec as P

MESH = pl.DeviceIdType.MESH
BLOCK = 128
HEAD = 128
ROWS = 512


def body(
    R,
    T,
    bt,
    cb,
    mreq,
    mdest,
    q_ref,
    kn_ref,
    vn_ref,
    kpool_hbm,
    vpool_hbm,
    levels_hbm,
    scale_ref,
    res_ref,
    gain_ref,
    hid_ref,
    norm_ref,
    rk_ref,
    rv_ref,
    cnt_ref,
    src_ref,
    kpool,
    vpool,
    levels,
    q16,
    stage,
    rx1,
    tx2,
    table,
    info_v,
    info_s,
    rs_tx,
    rs_rx,
    ss_tx,
    ss_rx,
    in_sem,
    mig_sem,
    meta_sem,
    info_sem,
    rs_sem,
    ss_sem,
):
    me = lax.axis_index("replica")
    tp = lax.axis_index("tp")
    CR = 2 * ROWS // R
    per_block = BLOCK // CR
    half = R // 2

    copies = [
        pltpu.make_async_copy(kpool_hbm, kpool, in_sem.at[0]),
        pltpu.make_async_copy(vpool_hbm, vpool, in_sem.at[1]),
        pltpu.make_async_copy(levels_hbm, levels, in_sem.at[2]),
    ]
    for c in copies:
        c.start()

    barrier = pltpu.get_barrier_semaphore()

    @pl.loop(1, R)
    def _(i):
        pl.semaphore_signal(
            barrier, inc=1, device_id={"replica": lax.rem(me + i, R)}, device_id_type=MESH
        )

    @pl.loop(1, T)
    def _(i):
        pl.semaphore_signal(
            barrier, inc=1, device_id={"tp": lax.rem(tp + i, T)}, device_id_type=MESH
        )

    lane = lax.broadcasted_iota(jnp.int32, (1, 128), 1)
    r0, r1 = mreq[0], mreq[1]
    c0, c1 = cb[r0], cb[r1]
    row = jnp.where(lane == mdest[0], me * 4 + c0, 0) + jnp.where(
        lane == 64 + mdest[1], me * 4 + c1, 0
    )
    table[me] = row
    copies[0].wait()
    copies[1].wait()
    for j, (r, c) in enumerate(((r0, c0), (r1, c1))):
        for kv, pool in enumerate((kpool, vpool)):
            for b in range(2):
                blk = pool[bt[b, r], 0]
                if b == 1:
                    blk = jnp.where(c > 1, blk, jnp.zeros_like(blk))
                at = (kv * 2 + b) * per_block
                stage[j, at : at + per_block] = blk.reshape(per_block, CR, HEAD)
    my_j = lax.rem(me, 2)
    my_t = me // 2
    rx1[me] = stage[my_j, my_t]

    pl.semaphore_wait(barrier, R + T - 2)

    @pl.loop(1, R)
    def _(i):
        to = lax.rem(me + i, R)
        pltpu.make_async_remote_copy(
            src_ref=table.at[me],
            dst_ref=table.at[me],
            send_sem=meta_sem.at[0],
            recv_sem=meta_sem.at[1],
            device_id={"replica": to},
            device_id_type=MESH,
        ).start()
        pltpu.make_async_remote_copy(
            src_ref=stage.at[lax.rem(to, 2), to // 2],
            dst_ref=rx1.at[me],
            send_sem=mig_sem.at[0],
            recv_sem=mig_sem.at[1],
            device_id={"replica": to},
            device_id_type=MESH,
        ).start()

    for h in range(4):
        for i in range(4):
            q16[4 * h + i : 4 * h + i + 1, :] = q_ref[i, h : h + 1, :].astype(jnp.float32)
    q = q16[...].astype(jnp.bfloat16)
    kn, vn = kn_ref[...], vn_ref[...]
    sm = 1.0 / math.sqrt(HEAD)
    keys = kpool[...].reshape(8 * BLOCK, HEAD)
    dims = (((1,), (1,)), ((), ()))
    scores = lax.dot_general(q, keys, dims, preferred_element_type=jnp.float32) * sm
    own4 = lax.dot_general(q, kn, dims, preferred_element_type=jnp.float32) * sm
    req = lax.rem(lax.broadcasted_iota(jnp.int32, (16, 1), 0), 4)
    first, second = jnp.full((16, 1), -1, jnp.int32), jnp.full((16, 1), -1, jnp.int32)
    for i in range(4):
        first = jnp.where(req == i, bt[0, i], first)
        second = jnp.where(req == i, jnp.where(cb[i] > 1, bt[1, i], -1), second)
    column = lax.broadcasted_iota(jnp.int32, (16, 8 * BLOCK), 1) // BLOCK
    live = (column == first) | (column == second)
    mine = lax.broadcasted_iota(jnp.int32, (16, 4), 1) == req
    own = jnp.sum(jnp.where(mine, own4, 0.0), axis=1, keepdims=True)
    masked = jnp.where(live, scores, jnp.float32(-1e30))
    top = jnp.maximum(jnp.max(masked, axis=1, keepdims=True), own)
    expo = jnp.where(live, jnp.exp(masked - top), 0.0)
    self_expo = jnp.exp(own - top)
    total = jnp.sum(expo, axis=1, keepdims=True) + self_expo
    weights = (expo / total).astype(jnp.bfloat16)
    self_weight = jnp.where(mine, self_expo / total, 0.0).astype(jnp.bfloat16)
    mixed = jnp.dot(
        weights, vpool[...].reshape(8 * BLOCK, HEAD), preferred_element_type=jnp.float32
    ) + jnp.dot(self_weight, vn, preferred_element_type=jnp.float32)
    attn = jnp.concatenate([mixed[4 * h : 4 * h + 4] for h in range(4)], axis=1).astype(
        jnp.bfloat16
    )

    pltpu.make_async_copy(
        table.at[pl.ds(0, R - 1)], table.at[pl.ds(0, R - 1)], meta_sem.at[1]
    ).wait()
    info_v[...] = jnp.sum(table[...], axis=0)
    info_copy = pltpu.make_async_copy(info_v, info_s, info_sem)
    info_copy.start()

    copies[2].wait()
    CW = levels.shape[1] // T

    @pl.loop(0, T)
    def _(i):
        to = lax.rem(tp + 1 + i, T)
        part = jnp.dot(
            attn,
            levels[:, pl.ds(pl.multiple_of(to * CW, CW), CW)],
            preferred_element_type=jnp.float32,
        )
        piece = jnp.concatenate(
            [part[:, 128 * k : 128 * k + 128] for k in range(CW // 128)], axis=0
        )
        rs_tx[to] = piece.astype(jnp.bfloat16)

        @pl.when(i < T - 1)
        def _():
            pltpu.make_async_remote_copy(
                src_ref=rs_tx.at[to],
                dst_ref=rs_rx.at[tp],
                send_sem=rs_sem.at[0],
                recv_sem=rs_sem.at[1],
                device_id={"tp": to},
                device_id_type=MESH,
            ).start()

    rs_rx[tp] = rs_tx[tp]

    info_copy.wait()
    pltpu.make_async_copy(
        rx1.at[pl.ds(0, R - 1)], rx1.at[pl.ds(0, R - 1)], mig_sem.at[1]
    ).wait()
    my_b = lax.rem(my_t // per_block, 2)
    my_k = lax.rem(my_t, per_block)

    def deliver(out):
        @pl.loop(1, R)
        def _(i):
            to = lax.rem(me + i, R)
            tx2[to] = rx1[lax.rem(info_s[0, 64 * my_j + to] // 4, R)]
            pltpu.make_async_remote_copy(
                src_ref=tx2.at[to],
                dst_ref=out.at[my_j, my_b, 0, my_k],
                send_sem=mig_sem.at[2],
                recv_sem=mig_sem.at[3],
                device_id={"replica": to},
                device_id_type=MESH,
            ).start()

        out[my_j, my_b, 0, my_k] = rx1[lax.rem(info_s[0, 64 * my_j + me] // 4, R)]

    @pl.when(my_t < half // 2)
    def _():
        deliver(rk_ref)

    @pl.when(my_t >= half // 2)
    def _():
        deliver(rv_ref)

    for j in range(2):
        word = info_s[0, 64 * j + me]
        src_ref[j] = word // 4
        cnt_ref[j] = lax.rem(word, 4)

    pltpu.make_async_copy(
        rs_rx.at[pl.ds(0, T - 1)], rs_rx.at[pl.ds(0, T - 1)], rs_sem.at[1]
    ).wait()
    sixteen = jnp.sum(rs_rx[...].astype(jnp.float32), axis=0)
    summed = jnp.concatenate([sixteen[4 * k : 4 * k + 4] for k in range(CW // 128)], axis=1)
    hidden = (summed * scale_ref[...] + res_ref[...].astype(jnp.float32)).astype(jnp.bfloat16)
    hid_ref[...] = hidden
    wide = hidden.astype(jnp.float32)
    square = jnp.sum(wide * wide, axis=1, keepdims=True)
    ss_tx[...] = jnp.broadcast_to(square, (4, 128))
    ss_rx[tp] = ss_tx[...]

    @pl.loop(1, T)
    def _(i):
        pltpu.make_async_remote_copy(
            src_ref=ss_tx,
            dst_ref=ss_rx.at[tp],
            send_sem=ss_sem.at[0],
            recv_sem=ss_sem.at[1],
            device_id={"tp": lax.rem(tp + i, T)},
            device_id_type=MESH,
        ).start()

    pltpu.make_async_copy(
        ss_rx.at[pl.ds(0, T - 1)], ss_rx.at[pl.ds(0, T - 1)], ss_sem.at[1]
    ).wait()
    mean = jnp.sum(ss_rx[...], axis=0)[:, 0:1] / (CW * T)
    norm_ref[...] = (wide * lax.rsqrt(mean + 1e-5) * gain_ref[...]).astype(jnp.bfloat16)

    @pl.when(my_j >= 0)
    def _():
        for buf, count, sem in (
            (rx1, R - 1, mig_sem.at[0]),
            (rx1, R - 1, mig_sem.at[2]),
            (rx1, R - 1, mig_sem.at[3]),
            (table, R - 1, meta_sem.at[0]),
            (rs_tx, T - 1, rs_sem.at[0]),
            (ss_rx, T - 1, ss_sem.at[0]),
        ):
            pltpu.make_async_copy(buf.at[pl.ds(0, count)], buf.at[pl.ds(0, count)], sem).wait()


def solution(mesh):
    R, T = mesh.shape["replica"], mesh.shape["tp"]
    CR = 2 * ROWS // R
    per_block = BLOCK // CR

    def shards(q, kn, vn, kpool, vpool, bt, cb, mreq, mdest, levels, scale, res, gain):
        CW = levels.shape[1] // T
        vmem = pl.BlockSpec(memory_space=pltpu.VMEM)
        smem = pl.BlockSpec(memory_space=pltpu.SMEM)
        anyspace = pl.BlockSpec(memory_space=pl.ANY)
        moved = (2, 2, 1, per_block, CR, HEAD)
        bf16, f32, i32 = jnp.bfloat16, jnp.float32, jnp.int32
        hid, norm, rk, rv, cnt, src = pl.pallas_call(
            functools.partial(body, R, T),
            out_shape=(
                jax.ShapeDtypeStruct((4, CW), bf16),
                jax.ShapeDtypeStruct((4, CW), bf16),
                jax.ShapeDtypeStruct(moved, bf16),
                jax.ShapeDtypeStruct(moved, bf16),
                jax.ShapeDtypeStruct((2,), i32),
                jax.ShapeDtypeStruct((2,), i32),
            ),
            in_specs=[smem] * 4 + [vmem] * 3 + [anyspace] * 3 + [vmem] * 3,
            out_specs=(vmem, vmem, vmem, vmem, smem, smem),
            scratch_shapes=[
                pltpu.VMEM((8, 1, BLOCK, HEAD), bf16),
                pltpu.VMEM((8, 1, BLOCK, HEAD), bf16),
                pltpu.VMEM(levels.shape, bf16),
                pltpu.VMEM((16, HEAD), f32),
                pltpu.VMEM((2, R // 2, CR, HEAD), bf16),
                pltpu.VMEM((R, CR, HEAD), bf16),
                pltpu.VMEM((R, CR, HEAD), bf16),
                pltpu.VMEM((R, 1, 128), i32),
                pltpu.VMEM((1, 128), i32),
                pltpu.SMEM((1, 128), i32),
                pltpu.VMEM((T, 4 * CW // 128, 128), bf16),
                pltpu.VMEM((T, 4 * CW // 128, 128), bf16),
                pltpu.VMEM((4, 128), f32),
                pltpu.VMEM((T, 4, 128), f32),
                pltpu.SemaphoreType.DMA((3,)),
                pltpu.SemaphoreType.DMA((4,)),
                pltpu.SemaphoreType.DMA((2,)),
                pltpu.SemaphoreType.DMA,
                pltpu.SemaphoreType.DMA((2,)),
                pltpu.SemaphoreType.DMA((2,)),
            ],
            compiler_params=pltpu.CompilerParams(
                collective_id=0, has_side_effects=True, vmem_limit_bytes=48 * 1024 * 1024
            ),
            name="decode_and_migrate",
        )(
            bt.T,
            cb,
            mreq,
            mdest,
            q,
            kn.reshape(4, HEAD),
            vn.reshape(4, HEAD),
            kpool,
            vpool,
            levels,
            scale[None, :],
            res,
            gain[None, :],
        )
        shape = (2, 2, 1, BLOCK, HEAD)
        return hid, norm, rk.reshape(shape), rv.reshape(shape), cnt, src

    return jax.shard_map(
        shards,
        mesh=mesh,
        in_specs=(
            P("replica", "tp", None),
            P("replica", "tp", None),
            P("replica", "tp", None),
            P("replica", "tp", None, None),
            P("replica", "tp", None, None),
            P("replica", None),
            P("replica"),
            P("replica"),
            P("replica"),
            P("tp", None),
            P("tp"),
            P("replica", "tp"),
            P("tp"),
        ),
        out_specs=(
            P("replica", "tp"),
            P("replica", "tp"),
            P("replica", None, "tp", None, None),
            P("replica", None, "tp", None, None),
            P("replica"),
            P("replica"),
        ),
        check_vma=False,
    )
```

```python
import functools
import math

import jax
import jax.numpy as jnp
from jax import lax
from jax.experimental import pallas as pl
from jax.experimental.pallas import tpu as pltpu
from jax.sharding import PartitionSpec as P

MESH = pl.DeviceIdType.MESH
BLOCK = 128
HEAD = 128
ROWS = 512


def body(
    R,
    T,
    bt_hbm,
    cb_hbm,
    mreq_hbm,
    mdest_hbm,
    kpool_hbm,
    vpool_hbm,
    q_hbm,
    kn_hbm,
    vn_hbm,
    levels_hbm,
    scale_hbm,
    res_hbm,
    gain_hbm,
    hid_out,
    norm_out,
    rk_ref,
    rv_ref,
    cnt_out,
    src_out,
    bt,
    cb,
    mreq,
    mdest,
    kpool,
    vpool,
    q_ref,
    kn_ref,
    vn_ref,
    levels,
    scale_ref,
    res_ref,
    gain_ref,
    cnt_ref,
    src_ref,
    hid_ref,
    norm_ref,
    q16,
    stage,
    rx1,
    tx2,
    table,
    info_v,
    info_s,
    rs_tx,
    rs_rx,
    ss_tx,
    ss_rx,
    in_sem,
    mig_sem,
    meta_sem,
    info_sem,
    rs_sem,
    ss_sem,
    out_sem,
):
    me = lax.axis_index("replica")
    tp = lax.axis_index("tp")
    CR = 2 * ROWS // R
    per_block = BLOCK // CR
    half = R // 2

    copies = [
        pltpu.make_async_copy(src, dst, in_sem.at[n])
        for n, (src, dst) in enumerate(
            (
                (bt_hbm, bt),
                (cb_hbm, cb),
                (mreq_hbm, mreq),
                (mdest_hbm, mdest),
                (kpool_hbm, kpool),
                (vpool_hbm, vpool),
                (q_hbm, q_ref),
                (kn_hbm, kn_ref),
                (vn_hbm, vn_ref),
                (levels_hbm, levels),
                (scale_hbm, scale_ref),
                (res_hbm, res_ref),
                (gain_hbm, gain_ref),
            )
        )
    ]
    for c in copies[:6]:
        c.start()

    barrier = pltpu.get_barrier_semaphore()

    @pl.loop(1, R)
    def _(i):
        pl.semaphore_signal(
            barrier, inc=1, device_id={"replica": lax.rem(me + i, R)}, device_id_type=MESH
        )

    @pl.loop(1, T)
    def _(i):
        pl.semaphore_signal(
            barrier, inc=1, device_id={"tp": lax.rem(tp + i, T)}, device_id_type=MESH
        )

    for c in copies[6:]:
        c.start()
    for c in copies[:4]:
        c.wait()

    lane = lax.broadcasted_iota(jnp.int32, (1, 128), 1)
    r0, r1 = mreq[0], mreq[1]
    c0, c1 = cb[r0], cb[r1]
    row = jnp.where(lane == mdest[0], me * 4 + c0, 0) + jnp.where(
        lane == 64 + mdest[1], me * 4 + c1, 0
    )
    table[me] = row
    copies[4].wait()
    copies[5].wait()
    for j, (r, c) in enumerate(((r0, c0), (r1, c1))):
        for kv, pool in enumerate((kpool, vpool)):
            for b in range(2):
                blk = pool[bt[b, r], 0]
                if b == 1:
                    blk = jnp.where(c > 1, blk, jnp.zeros_like(blk))
                at = (kv * 2 + b) * per_block
                stage[j, at : at + per_block] = blk.reshape(per_block, CR, HEAD)
    my_j = lax.rem(me, 2)
    my_t = me // 2
    rx1[me] = stage[my_j, my_t]

    pl.semaphore_wait(barrier, R + T - 2)

    @pl.loop(1, R)
    def _(i):
        to = lax.rem(me + i, R)
        pltpu.make_async_remote_copy(
            src_ref=table.at[me],
            dst_ref=table.at[me],
            send_sem=meta_sem.at[0],
            recv_sem=meta_sem.at[1],
            device_id={"replica": to},
            device_id_type=MESH,
        ).start()
        pltpu.make_async_remote_copy(
            src_ref=stage.at[lax.rem(to, 2), to // 2],
            dst_ref=rx1.at[me],
            send_sem=mig_sem.at[0],
            recv_sem=mig_sem.at[1],
            device_id={"replica": to},
            device_id_type=MESH,
        ).start()

    for c in copies[6:9]:
        c.wait()

    for h in range(4):
        for i in range(4):
            q16[4 * h + i : 4 * h + i + 1, :] = q_ref[i, h : h + 1, :].astype(jnp.float32)
    q = q16[...].astype(jnp.bfloat16)
    kn, vn = kn_ref[...], vn_ref[...]
    sm = 1.0 / math.sqrt(HEAD)
    keys = kpool[...].reshape(8 * BLOCK, HEAD)
    dims = (((1,), (1,)), ((), ()))
    scores = lax.dot_general(q, keys, dims, preferred_element_type=jnp.float32) * sm
    own4 = lax.dot_general(q, kn, dims, preferred_element_type=jnp.float32) * sm
    req = lax.rem(lax.broadcasted_iota(jnp.int32, (16, 1), 0), 4)
    first, second = jnp.full((16, 1), -1, jnp.int32), jnp.full((16, 1), -1, jnp.int32)
    for i in range(4):
        first = jnp.where(req == i, bt[0, i], first)
        second = jnp.where(req == i, jnp.where(cb[i] > 1, bt[1, i], -1), second)
    column = lax.broadcasted_iota(jnp.int32, (16, 8 * BLOCK), 1) // BLOCK
    live = (column == first) | (column == second)
    mine = lax.broadcasted_iota(jnp.int32, (16, 4), 1) == req
    own = jnp.sum(jnp.where(mine, own4, 0.0), axis=1, keepdims=True)
    masked = jnp.where(live, scores, jnp.float32(-1e30))
    top = jnp.maximum(jnp.max(masked, axis=1, keepdims=True), own)
    expo = jnp.where(live, jnp.exp(masked - top), 0.0)
    self_expo = jnp.exp(own - top)
    total = jnp.sum(expo, axis=1, keepdims=True) + self_expo
    weights = (expo / total).astype(jnp.bfloat16)
    self_weight = jnp.where(mine, self_expo / total, 0.0).astype(jnp.bfloat16)
    mixed = jnp.dot(
        weights, vpool[...].reshape(8 * BLOCK, HEAD), preferred_element_type=jnp.float32
    ) + jnp.dot(self_weight, vn, preferred_element_type=jnp.float32)
    attn = jnp.concatenate([mixed[4 * h : 4 * h + 4] for h in range(4)], axis=1).astype(
        jnp.bfloat16
    )

    pltpu.make_async_copy(
        table.at[pl.ds(0, R - 1)], table.at[pl.ds(0, R - 1)], meta_sem.at[1]
    ).wait()
    info_v[...] = jnp.sum(table[...], axis=0)
    info_copy = pltpu.make_async_copy(info_v, info_s, info_sem)
    info_copy.start()

    copies[9].wait()
    CW = levels.shape[1] // T

    @pl.loop(0, T)
    def _(i):
        to = lax.rem(tp + 1 + i, T)
        part = jnp.dot(
            attn,
            levels[:, pl.ds(pl.multiple_of(to * CW, CW), CW)],
            preferred_element_type=jnp.float32,
        )
        piece = jnp.concatenate(
            [part[:, 128 * k : 128 * k + 128] for k in range(CW // 128)], axis=0
        )
        rs_tx[to] = piece.astype(jnp.bfloat16)

        @pl.when(i < T - 1)
        def _():
            pltpu.make_async_remote_copy(
                src_ref=rs_tx.at[to],
                dst_ref=rs_rx.at[tp],
                send_sem=rs_sem.at[0],
                recv_sem=rs_sem.at[1],
                device_id={"tp": to},
                device_id_type=MESH,
            ).start()

    rs_rx[tp] = rs_tx[tp]

    info_copy.wait()
    pltpu.make_async_copy(
        rx1.at[pl.ds(0, R - 1)], rx1.at[pl.ds(0, R - 1)], mig_sem.at[1]
    ).wait()
    my_b = lax.rem(my_t // per_block, 2)
    my_k = lax.rem(my_t, per_block)

    def deliver(out):
        @pl.loop(1, R)
        def _(i):
            to = lax.rem(me + i, R)
            tx2[to] = rx1[lax.rem(info_s[0, 64 * my_j + to] // 4, R)]
            pltpu.make_async_remote_copy(
                src_ref=tx2.at[to],
                dst_ref=out.at[my_j, my_b, 0, my_k],
                send_sem=mig_sem.at[2],
                recv_sem=mig_sem.at[3],
                device_id={"replica": to},
                device_id_type=MESH,
            ).start()

        tx2[me] = rx1[lax.rem(info_s[0, 64 * my_j + me] // 4, R)]
        pltpu.make_async_copy(tx2.at[me], out.at[my_j, my_b, 0, my_k], out_sem.at[4]).start()

    @pl.when(my_t < half // 2)
    def _():
        deliver(rk_ref)

    @pl.when(my_t >= half // 2)
    def _():
        deliver(rv_ref)

    for j in range(2):
        word = info_s[0, 64 * j + me]
        src_ref[j] = word // 4
        cnt_ref[j] = lax.rem(word, 4)
    small = [
        pltpu.make_async_copy(cnt_ref, cnt_out, out_sem.at[0]),
        pltpu.make_async_copy(src_ref, src_out, out_sem.at[1]),
    ]
    for c in small:
        c.start()
    for c in copies[10:]:
        c.wait()

    pltpu.make_async_copy(
        rs_rx.at[pl.ds(0, T - 1)], rs_rx.at[pl.ds(0, T - 1)], rs_sem.at[1]
    ).wait()
    sixteen = jnp.sum(rs_rx[...].astype(jnp.float32), axis=0)
    summed = jnp.concatenate([sixteen[4 * k : 4 * k + 4] for k in range(CW // 128)], axis=1)
    hidden = (summed * scale_ref[...] + res_ref[...].astype(jnp.float32)).astype(jnp.bfloat16)
    hid_ref[...] = hidden
    small.append(pltpu.make_async_copy(hid_ref, hid_out, out_sem.at[2]))
    small[-1].start()
    wide = hidden.astype(jnp.float32)
    square = jnp.sum(wide * wide, axis=1, keepdims=True)
    ss_tx[...] = jnp.broadcast_to(square, (4, 128))
    ss_rx[tp] = ss_tx[...]

    @pl.loop(1, T)
    def _(i):
        pltpu.make_async_remote_copy(
            src_ref=ss_tx,
            dst_ref=ss_rx.at[tp],
            send_sem=ss_sem.at[0],
            recv_sem=ss_sem.at[1],
            device_id={"tp": lax.rem(tp + i, T)},
            device_id_type=MESH,
        ).start()

    pltpu.make_async_copy(
        ss_rx.at[pl.ds(0, T - 1)], ss_rx.at[pl.ds(0, T - 1)], ss_sem.at[1]
    ).wait()
    mean = jnp.sum(ss_rx[...], axis=0)[:, 0:1] / (CW * T)
    norm_ref[...] = (wide * lax.rsqrt(mean + 1e-5) * gain_ref[...]).astype(jnp.bfloat16)

    small.append(pltpu.make_async_copy(norm_ref, norm_out, out_sem.at[3]))
    small[-1].start()

    for c in small:
        c.wait()
    pltpu.make_async_copy(tx2.at[0], rk_ref.at[0, 0, 0, 0], out_sem.at[4]).wait()
    for buf, count, sem in (
        (rx1, R - 1, mig_sem.at[0]),
        (rx1, R - 1, mig_sem.at[2]),
        (rx1, R - 1, mig_sem.at[3]),
        (table, R - 1, meta_sem.at[0]),
        (rs_tx, T - 1, rs_sem.at[0]),
        (ss_rx, T - 1, ss_sem.at[0]),
    ):
        pltpu.make_async_copy(buf.at[pl.ds(0, count)], buf.at[pl.ds(0, count)], sem).wait()


def emit(n, *refs):
    ins, outs, held, sem = refs[:n], refs[n : 2 * n], refs[2 * n : 3 * n], refs[3 * n]
    loads = [pltpu.make_async_copy(ins[i], held[i], sem.at[0, i]) for i in range(n)]
    stores = [pltpu.make_async_copy(held[i], outs[i], sem.at[1, i]) for i in range(n)]
    for c in loads:
        c.start()
    for c, d in zip(loads, stores):
        c.wait()
        d.start()
    for c in stores:
        c.wait()


def solution(mesh):
    R, T = mesh.shape["replica"], mesh.shape["tp"]
    CR = 2 * ROWS // R
    per_block = BLOCK // CR

    def shards(q, kn, vn, kpool, vpool, bt, cb, mreq, mdest, levels, scale, res, gain):
        CW = levels.shape[1] // T
        vmem = pl.BlockSpec(memory_space=pltpu.VMEM)
        hbm = pl.BlockSpec(memory_space=pltpu.HBM)
        moved = (2, 2, 1, per_block, CR, HEAD)
        bf16, f32, i32 = jnp.bfloat16, jnp.float32, jnp.int32
        results = pl.pallas_call(
            functools.partial(body, R, T),
            out_shape=(
                jax.ShapeDtypeStruct((4, CW), bf16),
                jax.ShapeDtypeStruct((4, CW), bf16),
                jax.ShapeDtypeStruct(moved, bf16),
                jax.ShapeDtypeStruct(moved, bf16),
                jax.ShapeDtypeStruct((2,), i32),
                jax.ShapeDtypeStruct((2,), i32),
            ),
            in_specs=[hbm] * 13,
            out_specs=(hbm,) * 6,
            scratch_shapes=[
                pltpu.SMEM((2, 4), i32),
                pltpu.SMEM((4,), i32),
                pltpu.SMEM((2,), i32),
                pltpu.SMEM((2,), i32),
                pltpu.VMEM((8, 1, BLOCK, HEAD), bf16),
                pltpu.VMEM((8, 1, BLOCK, HEAD), bf16),
                pltpu.VMEM((4, 4, HEAD), bf16),
                pltpu.VMEM((4, HEAD), bf16),
                pltpu.VMEM((4, HEAD), bf16),
                pltpu.VMEM(levels.shape, bf16),
                pltpu.VMEM((1, CW), f32),
                pltpu.VMEM((4, CW), bf16),
                pltpu.VMEM((1, CW), f32),
                pltpu.SMEM((2,), i32),
                pltpu.SMEM((2,), i32),
                pltpu.VMEM((4, CW), bf16),
                pltpu.VMEM((4, CW), bf16),
                pltpu.VMEM((16, HEAD), f32),
                pltpu.VMEM((2, R // 2, CR, HEAD), bf16),
                pltpu.VMEM((R, CR, HEAD), bf16),
                pltpu.VMEM((R, CR, HEAD), bf16),
                pltpu.VMEM((R, 1, 128), i32),
                pltpu.VMEM((1, 128), i32),
                pltpu.SMEM((1, 128), i32),
                pltpu.VMEM((T, 4 * CW // 128, 128), bf16),
                pltpu.VMEM((T, 4 * CW // 128, 128), bf16),
                pltpu.VMEM((4, 128), f32),
                pltpu.VMEM((T, 4, 128), f32),
                pltpu.SemaphoreType.DMA((13,)),
                pltpu.SemaphoreType.DMA((4,)),
                pltpu.SemaphoreType.DMA((2,)),
                pltpu.SemaphoreType.DMA,
                pltpu.SemaphoreType.DMA((2,)),
                pltpu.SemaphoreType.DMA((2,)),
                pltpu.SemaphoreType.DMA((5,)),
            ],
            compiler_params=pltpu.CompilerParams(
                collective_id=0, has_side_effects=True, vmem_limit_bytes=60 * 1024 * 1024
            ),
            name="decode_and_migrate",
        )(
            bt.T,
            cb,
            mreq,
            mdest,
            kpool,
            vpool,
            q,
            kn.reshape(4, HEAD),
            vn.reshape(4, HEAD),
            levels,
            scale[None, :],
            res,
            gain[None, :],
        )
        hid, norm, rk, rv, cnt, src = pl.pallas_call(
            functools.partial(emit, 6),
            out_shape=tuple(jax.ShapeDtypeStruct(r.shape, r.dtype) for r in results),
            in_specs=[hbm] * 6,
            out_specs=(hbm,) * 6,
            scratch_shapes=[pltpu.VMEM(r.shape, r.dtype) for r in results]
            + [pltpu.SemaphoreType.DMA((2, 6))],
            compiler_params=pltpu.CompilerParams(vmem_limit_bytes=60 * 1024 * 1024),
            name="write_outputs",
        )(*results)
        shape = (2, 2, 1, BLOCK, HEAD)
        return hid, norm, rk.reshape(shape), rv.reshape(shape), cnt, src

    return jax.shard_map(
        shards,
        mesh=mesh,
        in_specs=(
            P("replica", "tp", None),
            P("replica", "tp", None),
            P("replica", "tp", None),
            P("replica", "tp", None, None),
            P("replica", "tp", None, None),
            P("replica", None),
            P("replica"),
            P("replica"),
            P("replica"),
            P("tp", None),
            P("tp"),
            P("replica", "tp"),
            P("tp"),
        ),
        out_specs=(
            P("replica", "tp"),
            P("replica", "tp"),
            P("replica", None, "tp", None, None),
            P("replica", None, "tp", None, None),
            P("replica"),
            P("replica"),
        ),
        check_vma=False,
    )
```

```python
import functools
import math

import jax
import jax.numpy as jnp
from jax import lax
from jax.experimental import pallas as pl
from jax.experimental.pallas import tpu as pltpu
from jax.sharding import PartitionSpec as P

MESH = pl.DeviceIdType.MESH
BLOCK = 128
HEAD = 128
ROWS = 512


def outward(centre, i):
    return jnp.where(lax.rem(i, 2) == 1, centre - (i + 1) // 2, centre + i // 2)


def spread(n):
    return sorted(range(n), key=lambda d: -min(d, n - d))


def body(
    R,
    T,
    bt_hbm,
    cb_hbm,
    mreq_hbm,
    mdest_hbm,
    kpool_hbm,
    vpool_hbm,
    q_hbm,
    kn_hbm,
    vn_hbm,
    levels_hbm,
    scale_hbm,
    res_hbm,
    gain_hbm,
    hid_out,
    norm_out,
    rk_ref,
    rv_ref,
    cnt_out,
    src_out,
    bt,
    cb,
    mreq,
    mdest,
    kpool,
    vpool,
    q_ref,
    kn_ref,
    vn_ref,
    levels,
    scale_ref,
    res_ref,
    gain_ref,
    cnt_ref,
    src_ref,
    hid_ref,
    norm_ref,
    q16,
    stage,
    rx1,
    tx2,
    table,
    info_v,
    info_s,
    rs_tx,
    rs_rx,
    ss_tx,
    ss_rx,
    in_sem,
    mig_sem,
    meta_sem,
    info_sem,
    rs_sem,
    ss_sem,
    out_sem,
):
    me = lax.axis_index("replica")
    tp = lax.axis_index("tp")
    CR = 2 * ROWS // R
    per_block = BLOCK // CR
    half = R // 2
    X = min(4, T)
    my_x = lax.rem(tp, X)
    Z = min(8, R // 2)
    Y = R // (2 * Z)
    my_y, my_z, core = me // (2 * Z), lax.rem(me // 2, Z), lax.rem(me, 2)

    ys = [lax.rem(my_y + d, Y) for d in spread(Y)]

    def plane(z):
        chips = [(y * Z + z) * 2 for y in ys]
        return [chip + c for chip in chips for c in (1 - core, core)]

    def farthest_first(i):
        return lax.rem(my_z + outward(Z // 2, i), Z)

    copies = [
        pltpu.make_async_copy(src, dst, in_sem.at[n])
        for n, (src, dst) in enumerate(
            (
                (bt_hbm, bt),
                (cb_hbm, cb),
                (mreq_hbm, mreq),
                (mdest_hbm, mdest),
                (kpool_hbm, kpool),
                (vpool_hbm, vpool),
                (q_hbm, q_ref),
                (kn_hbm, kn_ref),
                (vn_hbm, vn_ref),
                (levels_hbm, levels),
                (scale_hbm, scale_ref),
                (res_hbm, res_ref),
                (gain_hbm, gain_ref),
            )
        )
    ]
    for c in copies[:6]:
        c.start()

    barrier = pltpu.get_barrier_semaphore()

    def greet(to):
        pl.semaphore_signal(barrier, inc=1, device_id={"replica": to}, device_id_type=MESH)

    @pl.loop(0, Z)
    def _(i):
        peers = plane(farthest_first(i))
        for to in peers[:-1]:
            greet(to)

        @pl.when(i < Z - 1)
        def _():
            greet(peers[-1])

    @pl.loop(1, T)
    def _(i):
        pl.semaphore_signal(
            barrier, inc=1, device_id={"tp": lax.rem(tp + i, T)}, device_id_type=MESH
        )

    for c in copies[6:]:
        c.start()
    for c in copies[:4]:
        c.wait()

    lane = lax.broadcasted_iota(jnp.int32, (2, 128), 1)
    kind = lax.broadcasted_iota(jnp.int32, (2, 128), 0)
    r0, r1 = mreq[0], mreq[1]
    c0, c1 = cb[r0], cb[r1]
    table[me] = jnp.where(lane == mdest[0], jnp.where(kind == 0, me, c0), 0) + jnp.where(
        lane == 64 + mdest[1], jnp.where(kind == 0, me, c1), 0
    )
    copies[4].wait()
    copies[5].wait()
    for j, (r, c) in enumerate(((r0, c0), (r1, c1))):
        for kv, pool in enumerate((kpool, vpool)):
            for b in range(2):
                blk = pool[bt[b, r], 0]
                if b == 1:
                    blk = jnp.where(c > 1, blk, jnp.zeros_like(blk))
                at = (kv * 2 + b) * per_block
                stage[j, at : at + per_block] = blk.reshape(per_block, CR, HEAD)
    my_j = lax.rem(me, 2)
    my_t = me // 2
    rx1[me] = stage[my_j, my_t]

    CW = levels.shape[1] // T

    def compute():
        for c in copies[6:9]:
            c.wait()

        for h in range(4):
            for i in range(4):
                q16[4 * h + i : 4 * h + i + 1, :] = q_ref[i, h : h + 1, :].astype(jnp.float32)
        q = q16[...].astype(jnp.bfloat16)
        kn, vn = kn_ref[...], vn_ref[...]
        sm = 1.0 / math.sqrt(HEAD)
        keys = kpool[...].reshape(8 * BLOCK, HEAD)
        dims = (((1,), (1,)), ((), ()))
        scores = lax.dot_general(q, keys, dims, preferred_element_type=jnp.float32) * sm
        own4 = lax.dot_general(q, kn, dims, preferred_element_type=jnp.float32) * sm
        req = lax.rem(lax.broadcasted_iota(jnp.int32, (16, 1), 0), 4)
        first, second = jnp.full((16, 1), -1, jnp.int32), jnp.full((16, 1), -1, jnp.int32)
        for i in range(4):
            first = jnp.where(req == i, bt[0, i], first)
            second = jnp.where(req == i, jnp.where(cb[i] > 1, bt[1, i], -1), second)
        column = lax.broadcasted_iota(jnp.int32, (16, 8 * BLOCK), 1) // BLOCK
        live = (column == first) | (column == second)
        mine = lax.broadcasted_iota(jnp.int32, (16, 4), 1) == req
        own = jnp.sum(jnp.where(mine, own4, 0.0), axis=1, keepdims=True)
        masked = jnp.where(live, scores, jnp.float32(-1e30))
        top = jnp.maximum(jnp.max(masked, axis=1, keepdims=True), own)
        expo = jnp.where(live, jnp.exp(masked - top), 0.0)
        self_expo = jnp.exp(own - top)
        total = jnp.sum(expo, axis=1, keepdims=True) + self_expo
        weights = (expo / total).astype(jnp.bfloat16)
        self_weight = jnp.where(mine, self_expo / total, 0.0).astype(jnp.bfloat16)
        mixed = jnp.dot(
            weights, vpool[...].reshape(8 * BLOCK, HEAD), preferred_element_type=jnp.float32
        ) + jnp.dot(self_weight, vn, preferred_element_type=jnp.float32)
        attn = jnp.concatenate([mixed[4 * h : 4 * h + 4] for h in range(4)], axis=1).astype(
            jnp.bfloat16
        )

        copies[9].wait()

        @pl.loop(0, T)
        def _(to):
            part = jnp.dot(
                attn,
                levels[:, pl.ds(pl.multiple_of(to * CW, CW), CW)],
                preferred_element_type=jnp.float32,
            )
            piece = jnp.concatenate(
                [part[:, 128 * k : 128 * k + 128] for k in range(CW // 128)], axis=0
            )
            rs_tx[to] = piece.astype(jnp.bfloat16)

    hid_copy = pltpu.make_async_copy(hid_ref, hid_out, out_sem.at[2])

    def reduce_scatter():
        rs_rx[tp] = rs_tx[tp]

        @pl.loop(1, T)
        def _(i):
            to = lax.rem(tp + i, T)
            pltpu.make_async_remote_copy(
                src_ref=rs_tx.at[to],
                dst_ref=rs_rx.at[tp],
                send_sem=rs_sem.at[0],
                recv_sem=rs_sem.at[1],
                device_id={"tp": to},
                device_id_type=MESH,
            ).start()

    def finish_hidden():
        for c in copies[10:]:
            c.wait()

        pltpu.make_async_copy(
            rs_rx.at[pl.ds(0, T - 1)], rs_rx.at[pl.ds(0, T - 1)], rs_sem.at[1]
        ).wait()
        sixteen = jnp.sum(rs_rx[...].astype(jnp.float32), axis=0)
        summed = jnp.concatenate([sixteen[4 * k : 4 * k + 4] for k in range(CW // 128)], axis=1)
        hidden = (summed * scale_ref[...] + res_ref[...].astype(jnp.float32)).astype(jnp.bfloat16)
        hid_ref[...] = hidden
        hid_copy.start()
        wide = hidden.astype(jnp.float32)
        square = jnp.sum(wide * wide, axis=1, keepdims=True)
        ss_tx[...] = jnp.broadcast_to(square, (4, 128))
        ss_rx[tp] = ss_tx[...]

        @pl.loop(1, T)
        def _(i):
            pltpu.make_async_remote_copy(
                src_ref=ss_tx,
                dst_ref=ss_rx.at[tp],
                send_sem=ss_sem.at[0],
                recv_sem=ss_sem.at[1],
                device_id={"tp": lax.rem(tp + i, T)},
                device_id_type=MESH,
            ).start()

    early = my_z < Z // 2
    pl.when(early)(compute)

    pl.semaphore_wait(barrier, R + T - 2)

    pl.when(early)(reduce_scatter)

    @pl.loop(0, R // X)
    def _(i):
        to = i * X + my_x

        @pl.when(to != me)
        def _():
            pltpu.make_async_remote_copy(
                src_ref=table.at[me],
                dst_ref=table.at[me],
                send_sem=meta_sem.at[0],
                recv_sem=meta_sem.at[1],
                device_id={"replica": to},
                device_id_type=MESH,
            ).start()

    def scatter(to):
        pltpu.make_async_remote_copy(
            src_ref=stage.at[lax.rem(to, 2), to // 2],
            dst_ref=rx1.at[me],
            send_sem=mig_sem.at[0],
            recv_sem=mig_sem.at[1],
            device_id={"replica": to},
            device_id_type=MESH,
        ).start()

    @pl.loop(0, Z)
    def _(i):
        peers = plane(farthest_first(i))
        for to in peers[:-1]:
            scatter(to)

        @pl.when(i < Z - 1)
        def _():
            scatter(peers[-1])

    @pl.when(jnp.logical_not(early))
    def _():
        compute()
        reduce_scatter()

    collects = lax.rem(me, X) == my_x

    @pl.when(collects)
    def _():
        pltpu.make_async_copy(
            table.at[pl.ds(0, R - 1)], table.at[pl.ds(0, R - 1)], meta_sem.at[1]
        ).wait()
        info_v[...] = jnp.minimum(jnp.sum(table[...], axis=0), R - 1)

        @pl.loop(1, X)
        def _(i):
            pltpu.make_async_remote_copy(
                src_ref=info_v,
                dst_ref=info_v,
                send_sem=info_sem.at[0],
                recv_sem=info_sem.at[1],
                device_id={"tp": tp - my_x + lax.rem(my_x + i, X)},
                device_id_type=MESH,
            ).start()

    pl.when(early)(finish_hidden)

    @pl.when(jnp.logical_not(collects))
    def _():
        pltpu.make_async_copy(info_v, info_v, info_sem.at[1]).wait()

    info_copy = pltpu.make_async_copy(info_v, info_s, info_sem.at[2])
    info_copy.start()

    info_copy.wait()
    pltpu.make_async_copy(
        rx1.at[pl.ds(0, R - 1)], rx1.at[pl.ds(0, R - 1)], mig_sem.at[1]
    ).wait()
    my_b = lax.rem(my_t // per_block, 2)
    my_k = lax.rem(my_t, per_block)

    def deliver(out):
        def send(to):
            pltpu.make_async_remote_copy(
                src_ref=tx2.at[to],
                dst_ref=out.at[my_j, my_b, 0, my_k],
                send_sem=mig_sem.at[2],
                recv_sem=mig_sem.at[3],
                device_id={"replica": to},
                device_id_type=MESH,
            ).start()

        @pl.loop(0, Z)
        def _(z):
            peers = plane(z)
            pieces = [rx1[info_s[0, 64 * my_j + to]] for to in peers]
            for to, piece in zip(peers, pieces):
                tx2[to] = piece
            for to in peers[:-1]:
                send(to)

            @pl.when(z != my_z)
            def _():
                send(peers[-1])

        pltpu.make_async_copy(tx2.at[me], out.at[my_j, my_b, 0, my_k], out_sem.at[4]).start()

    @pl.when(my_t < half // 2)
    def _():
        deliver(rk_ref)

    @pl.when(my_t >= half // 2)
    def _():
        deliver(rv_ref)

    for j in range(2):
        src_ref[j] = info_s[0, 64 * j + me]
        cnt_ref[j] = info_s[1, 64 * j + me]
    small = [
        pltpu.make_async_copy(cnt_ref, cnt_out, out_sem.at[0]),
        pltpu.make_async_copy(src_ref, src_out, out_sem.at[1]),
    ]
    for c in small:
        c.start()

    small.append(hid_copy)
    pl.when(jnp.logical_not(early))(finish_hidden)

    pltpu.make_async_copy(
        ss_rx.at[pl.ds(0, T - 1)], ss_rx.at[pl.ds(0, T - 1)], ss_sem.at[1]
    ).wait()
    wide = hid_ref[...].astype(jnp.float32)
    mean = jnp.sum(ss_rx[...], axis=0)[:, 0:1] / (CW * T)
    norm_ref[...] = (wide * lax.rsqrt(mean + 1e-5) * gain_ref[...]).astype(jnp.bfloat16)

    small.append(pltpu.make_async_copy(norm_ref, norm_out, out_sem.at[3]))
    small[-1].start()

    for c in small:
        c.wait()
    pltpu.make_async_copy(tx2.at[0], rk_ref.at[0, 0, 0, 0], out_sem.at[4]).wait()
    for buf, count, sem in (
        (rx1, R - 1, mig_sem.at[0]),
        (rx1, R - 1, mig_sem.at[2]),
        (rx1, R - 1, mig_sem.at[3]),
        (rs_tx, T - 1, rs_sem.at[0]),
        (ss_rx, T - 1, ss_sem.at[0]),
    ):
        pltpu.make_async_copy(buf.at[pl.ds(0, count)], buf.at[pl.ds(0, count)], sem).wait()

    @pl.when(collects)
    def _():
        for count, sem in ((R // X - 1, meta_sem.at[0]), (X - 1, info_sem.at[0])):
            pltpu.make_async_copy(table.at[pl.ds(0, count)], table.at[pl.ds(0, count)], sem).wait()

    @pl.when(jnp.logical_not(collects))
    def _():
        pltpu.make_async_copy(
            table.at[pl.ds(0, R // X)], table.at[pl.ds(0, R // X)], meta_sem.at[0]
        ).wait()


def emit(n, *refs):
    ins, outs, held, sem = refs[:n], refs[n : 2 * n], refs[2 * n : 3 * n], refs[3 * n]
    loads = [pltpu.make_async_copy(ins[i], held[i], sem.at[0, i]) for i in range(n)]
    stores = [pltpu.make_async_copy(held[i], outs[i], sem.at[1, i]) for i in range(n)]
    for c in loads:
        c.start()
    for c, d in zip(loads, stores):
        c.wait()
        d.start()
    for c in stores:
        c.wait()


def solution(mesh):
    R, T = mesh.shape["replica"], mesh.shape["tp"]
    CR = 2 * ROWS // R
    per_block = BLOCK // CR

    def shards(q, kn, vn, kpool, vpool, bt, cb, mreq, mdest, levels, scale, res, gain):
        CW = levels.shape[1] // T
        vmem = pl.BlockSpec(memory_space=pltpu.VMEM)
        hbm = pl.BlockSpec(memory_space=pltpu.HBM)
        moved = (2, 2, 1, per_block, CR, HEAD)
        bf16, f32, i32 = jnp.bfloat16, jnp.float32, jnp.int32
        results = pl.pallas_call(
            functools.partial(body, R, T),
            out_shape=(
                jax.ShapeDtypeStruct((4, CW), bf16),
                jax.ShapeDtypeStruct((4, CW), bf16),
                jax.ShapeDtypeStruct(moved, bf16),
                jax.ShapeDtypeStruct(moved, bf16),
                jax.ShapeDtypeStruct((2,), i32),
                jax.ShapeDtypeStruct((2,), i32),
            ),
            in_specs=[hbm] * 13,
            out_specs=(hbm,) * 6,
            scratch_shapes=[
                pltpu.SMEM((2, 4), i32),
                pltpu.SMEM((4,), i32),
                pltpu.SMEM((2,), i32),
                pltpu.SMEM((2,), i32),
                pltpu.VMEM((8, 1, BLOCK, HEAD), bf16),
                pltpu.VMEM((8, 1, BLOCK, HEAD), bf16),
                pltpu.VMEM((4, 4, HEAD), bf16),
                pltpu.VMEM((4, HEAD), bf16),
                pltpu.VMEM((4, HEAD), bf16),
                pltpu.VMEM(levels.shape, bf16),
                pltpu.VMEM((1, CW), f32),
                pltpu.VMEM((4, CW), bf16),
                pltpu.VMEM((1, CW), f32),
                pltpu.SMEM((2,), i32),
                pltpu.SMEM((2,), i32),
                pltpu.VMEM((4, CW), bf16),
                pltpu.VMEM((4, CW), bf16),
                pltpu.VMEM((16, HEAD), f32),
                pltpu.VMEM((2, R // 2, CR, HEAD), bf16),
                pltpu.VMEM((R, CR, HEAD), bf16),
                pltpu.VMEM((R, CR, HEAD), bf16),
                pltpu.VMEM((R, 2, 128), i32),
                pltpu.VMEM((2, 128), i32),
                pltpu.SMEM((2, 128), i32),
                pltpu.VMEM((T, 4 * CW // 128, 128), bf16),
                pltpu.VMEM((T, 4 * CW // 128, 128), bf16),
                pltpu.VMEM((4, 128), f32),
                pltpu.VMEM((T, 4, 128), f32),
                pltpu.SemaphoreType.DMA((13,)),
                pltpu.SemaphoreType.DMA((4,)),
                pltpu.SemaphoreType.DMA((2,)),
                pltpu.SemaphoreType.DMA((3,)),
                pltpu.SemaphoreType.DMA((2,)),
                pltpu.SemaphoreType.DMA((2,)),
                pltpu.SemaphoreType.DMA((5,)),
            ],
            compiler_params=pltpu.CompilerParams(
                collective_id=0, has_side_effects=True, vmem_limit_bytes=60 * 1024 * 1024
            ),
            name="decode_and_migrate",
        )(
            bt.T,
            cb,
            mreq,
            mdest,
            kpool,
            vpool,
            q,
            kn.reshape(4, HEAD),
            vn.reshape(4, HEAD),
            levels,
            scale[None, :],
            res,
            gain[None, :],
        )
        hid, norm, rk, rv, cnt, src = pl.pallas_call(
            functools.partial(emit, 6),
            out_shape=tuple(jax.ShapeDtypeStruct(r.shape, r.dtype) for r in results),
            in_specs=[hbm] * 6,
            out_specs=(hbm,) * 6,
            scratch_shapes=[pltpu.VMEM(r.shape, r.dtype) for r in results]
            + [pltpu.SemaphoreType.DMA((2, 6))],
            compiler_params=pltpu.CompilerParams(vmem_limit_bytes=60 * 1024 * 1024),
            name="write_outputs",
        )(*results)
        shape = (2, 2, 1, BLOCK, HEAD)
        return hid, norm, rk.reshape(shape), rv.reshape(shape), cnt, src

    return jax.shard_map(
        shards,
        mesh=mesh,
        in_specs=(
            P("replica", "tp", None),
            P("replica", "tp", None),
            P("replica", "tp", None),
            P("replica", "tp", None, None),
            P("replica", "tp", None, None),
            P("replica", None),
            P("replica"),
            P("replica"),
            P("replica"),
            P("tp", None),
            P("tp"),
            P("replica", "tp"),
            P("tp"),
        ),
        out_specs=(
            P("replica", "tp"),
            P("replica", "tp"),
            P("replica", None, "tp", None, None),
            P("replica", None, "tp", None, None),
            P("replica"),
            P("replica"),
        ),
        check_vma=False,
    )
```

```python
import functools
import math

import jax
import jax.numpy as jnp
from jax import lax
from jax.experimental import pallas as pl
from jax.experimental.pallas import tpu as pltpu
from jax.sharding import PartitionSpec as P

MESH = pl.DeviceIdType.MESH
BLOCK = 128
HEAD = 128
ROWS = 512


def outward(centre, i):
    return jnp.where(lax.rem(i, 2) == 1, centre - (i + 1) // 2, centre + i // 2)


def spread(n):
    return sorted(range(n), key=lambda d: -min(d, n - d))


def body(
    R,
    T,
    bt_hbm,
    cb_hbm,
    mreq_hbm,
    mdest_hbm,
    kpool_hbm,
    vpool_hbm,
    q_hbm,
    kn_hbm,
    vn_hbm,
    levels_hbm,
    scale_hbm,
    res_hbm,
    gain_hbm,
    hid_out,
    norm_out,
    rk_ref,
    rv_ref,
    cnt_out,
    src_out,
    bt,
    cb,
    mreq,
    mdest,
    kpool,
    vpool,
    q_ref,
    kn_ref,
    vn_ref,
    levels,
    scale_ref,
    res_ref,
    gain_ref,
    cnt_ref,
    src_ref,
    hid_ref,
    norm_ref,
    q16,
    stage,
    rx1,
    tx2,
    row,
    table,
    info,
    info_s,
    rs_tx,
    rs_rx,
    ss_tx,
    ss_rx,
    in_sem,
    mig_sem,
    meta_sem,
    info_sem,
    rs_sem,
    ss_sem,
    out_sem,
):
    me = lax.axis_index("replica")
    tp = lax.axis_index("tp")
    CR = 2 * ROWS // R
    per_block = BLOCK // CR
    half = R // 2
    Z = min(8, R // 2)
    Y = R // (2 * Z)
    my_y, my_z, core = me // (2 * Z), lax.rem(me // 2, Z), lax.rem(me, 2)

    ys = [lax.rem(my_y + d, Y) for d in spread(Y)]

    def plane(z):
        chips = [(y * Z + z) * 2 for y in ys]
        return [chip + c for chip in chips for c in (1 - core, core)]

    def farthest_first(i):
        return lax.rem(my_z + outward(Z // 2, i), Z)

    copies = [
        pltpu.make_async_copy(src, dst, in_sem.at[n])
        for n, (src, dst) in enumerate(
            (
                (bt_hbm, bt),
                (cb_hbm, cb),
                (mreq_hbm, mreq),
                (mdest_hbm, mdest),
                (kpool_hbm, kpool),
                (vpool_hbm, vpool),
                (q_hbm, q_ref),
                (kn_hbm, kn_ref),
                (vn_hbm, vn_ref),
                (levels_hbm, levels),
                (scale_hbm, scale_ref),
                (res_hbm, res_ref),
                (gain_hbm, gain_ref),
            )
        )
    ]
    for c in copies[:6]:
        c.start()

    barrier = pltpu.get_barrier_semaphore()

    def greet(to):
        pl.semaphore_signal(barrier, inc=1, device_id={"replica": to}, device_id_type=MESH)

    @pl.loop(0, Z)
    def _(i):
        peers = plane(farthest_first(i))
        for to in peers[:-1]:
            greet(to)

        @pl.when(i < Z - 1)
        def _():
            greet(peers[-1])

    @pl.loop(1, T)
    def _(i):
        pl.semaphore_signal(
            barrier, inc=1, device_id={"tp": lax.rem(tp + i, T)}, device_id_type=MESH
        )

    for c in copies[6:]:
        c.start()
    for c in copies[:4]:
        c.wait()

    lane = lax.broadcasted_iota(jnp.int32, (1, 128), 1)
    r0, r1 = mreq[0], mreq[1]
    c0, c1 = cb[r0], cb[r1]
    for j, c in enumerate((c0, c1)):
        row[j] = jnp.where(lane == mdest[j], me, 0) + jnp.where(lane == 64 + mdest[j], c, 0)
    table[me] = row[core]
    copies[4].wait()
    copies[5].wait()
    for j, (r, c) in enumerate(((r0, c0), (r1, c1))):
        for kv, pool in enumerate((kpool, vpool)):
            for b in range(2):
                blk = pool[bt[b, r], 0]
                if b == 1:
                    blk = jnp.where(c > 1, blk, jnp.zeros_like(blk))
                at = (kv * 2 + b) * per_block
                stage[j, at : at + per_block] = blk.reshape(per_block, CR, HEAD)
    my_j = lax.rem(me, 2)
    my_t = me // 2
    rx1[me] = stage[my_j, my_t]

    CW = levels.shape[1] // T

    def compute():
        for c in copies[6:9]:
            c.wait()

        for h in range(4):
            for i in range(4):
                q16[4 * h + i : 4 * h + i + 1, :] = q_ref[i, h : h + 1, :].astype(jnp.float32)
        q = q16[...].astype(jnp.bfloat16)
        kn, vn = kn_ref[...], vn_ref[...]
        sm = 1.0 / math.sqrt(HEAD)
        keys = kpool[...].reshape(8 * BLOCK, HEAD)
        dims = (((1,), (1,)), ((), ()))
        scores = lax.dot_general(q, keys, dims, preferred_element_type=jnp.float32) * sm
        own4 = lax.dot_general(q, kn, dims, preferred_element_type=jnp.float32) * sm
        req = lax.rem(lax.broadcasted_iota(jnp.int32, (16, 1), 0), 4)
        first, second = jnp.full((16, 1), -1, jnp.int32), jnp.full((16, 1), -1, jnp.int32)
        for i in range(4):
            first = jnp.where(req == i, bt[0, i], first)
            second = jnp.where(req == i, jnp.where(cb[i] > 1, bt[1, i], -1), second)
        column = lax.broadcasted_iota(jnp.int32, (16, 8 * BLOCK), 1) // BLOCK
        live = (column == first) | (column == second)
        mine = lax.broadcasted_iota(jnp.int32, (16, 4), 1) == req
        own = jnp.sum(jnp.where(mine, own4, 0.0), axis=1, keepdims=True)
        masked = jnp.where(live, scores, jnp.float32(-1e30))
        top = jnp.maximum(jnp.max(masked, axis=1, keepdims=True), own)
        expo = jnp.where(live, jnp.exp(masked - top), 0.0)
        self_expo = jnp.exp(own - top)
        total = jnp.sum(expo, axis=1, keepdims=True) + self_expo
        weights = (expo / total).astype(jnp.bfloat16)
        self_weight = jnp.where(mine, self_expo / total, 0.0).astype(jnp.bfloat16)
        mixed = jnp.dot(
            weights, vpool[...].reshape(8 * BLOCK, HEAD), preferred_element_type=jnp.float32
        ) + jnp.dot(self_weight, vn, preferred_element_type=jnp.float32)
        attn = jnp.concatenate([mixed[4 * h : 4 * h + 4] for h in range(4)], axis=1).astype(
            jnp.bfloat16
        )

        copies[9].wait()

        @pl.loop(0, T)
        def _(to):
            part = jnp.dot(
                attn,
                levels[:, pl.ds(pl.multiple_of(to * CW, CW), CW)],
                preferred_element_type=jnp.float32,
            )
            piece = jnp.concatenate(
                [part[:, 128 * k : 128 * k + 128] for k in range(CW // 128)], axis=0
            )
            rs_tx[to] = piece.astype(jnp.bfloat16)

    hid_copy = pltpu.make_async_copy(hid_ref, hid_out, out_sem.at[2])

    def reduce_scatter():
        rs_rx[tp] = rs_tx[tp]

        @pl.loop(1, T)
        def _(i):
            to = lax.rem(tp + i, T)
            pltpu.make_async_remote_copy(
                src_ref=rs_tx.at[to],
                dst_ref=rs_rx.at[tp],
                send_sem=rs_sem.at[0],
                recv_sem=rs_sem.at[1],
                device_id={"tp": to},
                device_id_type=MESH,
            ).start()

    def finish_hidden():
        for c in copies[10:]:
            c.wait()

        pltpu.make_async_copy(
            rs_rx.at[pl.ds(0, T - 1)], rs_rx.at[pl.ds(0, T - 1)], rs_sem.at[1]
        ).wait()
        sixteen = jnp.sum(rs_rx[...].astype(jnp.float32), axis=0)
        summed = jnp.concatenate([sixteen[4 * k : 4 * k + 4] for k in range(CW // 128)], axis=1)
        hidden = (summed * scale_ref[...] + res_ref[...].astype(jnp.float32)).astype(jnp.bfloat16)
        hid_ref[...] = hidden
        hid_copy.start()
        wide = hidden.astype(jnp.float32)
        square = jnp.sum(wide * wide, axis=1, keepdims=True)
        ss_tx[...] = jnp.broadcast_to(square, (4, 128))
        ss_rx[tp] = ss_tx[...]

        @pl.loop(1, T)
        def _(i):
            pltpu.make_async_remote_copy(
                src_ref=ss_tx,
                dst_ref=ss_rx.at[tp],
                send_sem=ss_sem.at[0],
                recv_sem=ss_sem.at[1],
                device_id={"tp": lax.rem(tp + i, T)},
                device_id_type=MESH,
            ).start()

    early = my_z < Z // 2
    pl.when(early)(compute)

    pl.semaphore_wait(barrier, R + T - 2)

    pl.when(early)(reduce_scatter)

    def announce(to):
        pltpu.make_async_remote_copy(
            src_ref=row.at[lax.rem(to, 2)],
            dst_ref=table.at[me],
            send_sem=meta_sem.at[0],
            recv_sem=meta_sem.at[1],
            device_id={"replica": to},
            device_id_type=MESH,
        ).start()

    def scatter(to):
        pltpu.make_async_remote_copy(
            src_ref=stage.at[lax.rem(to, 2), to // 2],
            dst_ref=rx1.at[me],
            send_sem=mig_sem.at[0],
            recv_sem=mig_sem.at[1],
            device_id={"replica": to},
            device_id_type=MESH,
        ).start()

    @pl.loop(0, Z)
    def _(i):
        peers = plane(farthest_first(i))
        for to in peers[:-1]:
            announce(to)

        @pl.when(i < Z - 1)
        def _():
            announce(peers[-1])

    @pl.loop(0, Z)
    def _(i):
        peers = plane(farthest_first(i))
        for to in peers[:-1]:
            scatter(to)

        @pl.when(i < Z - 1)
        def _():
            scatter(peers[-1])

    @pl.when(jnp.logical_not(early))
    def _():
        compute()
        reduce_scatter()

    pl.when(early)(finish_hidden)

    pltpu.make_async_copy(
        table.at[pl.ds(0, R - 1)], table.at[pl.ds(0, R - 1)], meta_sem.at[1]
    ).wait()
    info[0] = jnp.minimum(jnp.sum(table[...], axis=0), R - 1)
    info_copy = pltpu.make_async_copy(info.at[0], info_s.at[0], info_sem.at[0])
    info_copy.start()
    swap = pltpu.make_async_remote_copy(
        src_ref=info.at[0],
        dst_ref=info.at[1],
        send_sem=info_sem.at[1],
        recv_sem=info_sem.at[2],
        device_id={"replica": me + 1 - 2 * core},
        device_id_type=MESH,
    )
    swap.start()

    info_copy.wait()
    pltpu.make_async_copy(
        rx1.at[pl.ds(0, R - 1)], rx1.at[pl.ds(0, R - 1)], mig_sem.at[1]
    ).wait()
    my_b = lax.rem(my_t // per_block, 2)
    my_k = lax.rem(my_t, per_block)

    def deliver(out):
        def send(to):
            pltpu.make_async_remote_copy(
                src_ref=tx2.at[to],
                dst_ref=out.at[my_j, my_b, 0, my_k],
                send_sem=mig_sem.at[2],
                recv_sem=mig_sem.at[3],
                device_id={"replica": to},
                device_id_type=MESH,
            ).start()

        @pl.loop(0, Z)
        def _(z):
            peers = plane(z)
            pieces = [rx1[info_s[0, 0, to]] for to in peers]
            for to, piece in zip(peers, pieces):
                tx2[to] = piece
            for to in peers[:-1]:
                send(to)

            @pl.when(z != my_z)
            def _():
                send(peers[-1])

        pltpu.make_async_copy(tx2.at[me], out.at[my_j, my_b, 0, my_k], out_sem.at[4]).start()

    @pl.when(my_t < half // 2)
    def _():
        deliver(rk_ref)

    @pl.when(my_t >= half // 2)
    def _():
        deliver(rv_ref)

    swap.wait()
    swap_copy = pltpu.make_async_copy(info.at[1], info_s.at[1], info_sem.at[3])
    swap_copy.start()
    swap_copy.wait()
    for j in range(2):
        k = jnp.where(core == j, 0, 1)
        src_ref[j] = info_s[k, 0, me]
        cnt_ref[j] = info_s[k, 0, 64 + me]
    small = [
        pltpu.make_async_copy(cnt_ref, cnt_out, out_sem.at[0]),
        pltpu.make_async_copy(src_ref, src_out, out_sem.at[1]),
    ]
    for c in small:
        c.start()

    small.append(hid_copy)
    pl.when(jnp.logical_not(early))(finish_hidden)

    pltpu.make_async_copy(
        ss_rx.at[pl.ds(0, T - 1)], ss_rx.at[pl.ds(0, T - 1)], ss_sem.at[1]
    ).wait()
    wide = hid_ref[...].astype(jnp.float32)
    mean = jnp.sum(ss_rx[...], axis=0)[:, 0:1] / (CW * T)
    norm_ref[...] = (wide * lax.rsqrt(mean + 1e-5) * gain_ref[...]).astype(jnp.bfloat16)

    small.append(pltpu.make_async_copy(norm_ref, norm_out, out_sem.at[3]))
    small[-1].start()

    for c in small:
        c.wait()
    pltpu.make_async_copy(tx2.at[0], rk_ref.at[0, 0, 0, 0], out_sem.at[4]).wait()
    for buf, count, sem in (
        (rx1, R - 1, mig_sem.at[0]),
        (rx1, R - 1, mig_sem.at[2]),
        (rx1, R - 1, mig_sem.at[3]),
        (rs_tx, T - 1, rs_sem.at[0]),
        (ss_rx, T - 1, ss_sem.at[0]),
        (table, R - 1, meta_sem.at[0]),
    ):
        pltpu.make_async_copy(buf.at[pl.ds(0, count)], buf.at[pl.ds(0, count)], sem).wait()


def emit(n, *refs):
    ins, outs, held, sem = refs[:n], refs[n : 2 * n], refs[2 * n : 3 * n], refs[3 * n]
    loads = [pltpu.make_async_copy(ins[i], held[i], sem.at[0, i]) for i in range(n)]
    stores = [pltpu.make_async_copy(held[i], outs[i], sem.at[1, i]) for i in range(n)]
    for c in loads:
        c.start()
    for c, d in zip(loads, stores):
        c.wait()
        d.start()
    for c in stores:
        c.wait()


def solution(mesh):
    R, T = mesh.shape["replica"], mesh.shape["tp"]
    CR = 2 * ROWS // R
    per_block = BLOCK // CR

    def shards(q, kn, vn, kpool, vpool, bt, cb, mreq, mdest, levels, scale, res, gain):
        CW = levels.shape[1] // T
        vmem = pl.BlockSpec(memory_space=pltpu.VMEM)
        hbm = pl.BlockSpec(memory_space=pltpu.HBM)
        moved = (2, 2, 1, per_block, CR, HEAD)
        bf16, f32, i32 = jnp.bfloat16, jnp.float32, jnp.int32
        results = pl.pallas_call(
            functools.partial(body, R, T),
            out_shape=(
                jax.ShapeDtypeStruct((4, CW), bf16),
                jax.ShapeDtypeStruct((4, CW), bf16),
                jax.ShapeDtypeStruct(moved, bf16),
                jax.ShapeDtypeStruct(moved, bf16),
                jax.ShapeDtypeStruct((2,), i32),
                jax.ShapeDtypeStruct((2,), i32),
            ),
            in_specs=[hbm] * 13,
            out_specs=(hbm,) * 6,
            scratch_shapes=[
                pltpu.SMEM((2, 4), i32),
                pltpu.SMEM((4,), i32),
                pltpu.SMEM((2,), i32),
                pltpu.SMEM((2,), i32),
                pltpu.VMEM((8, 1, BLOCK, HEAD), bf16),
                pltpu.VMEM((8, 1, BLOCK, HEAD), bf16),
                pltpu.VMEM((4, 4, HEAD), bf16),
                pltpu.VMEM((4, HEAD), bf16),
                pltpu.VMEM((4, HEAD), bf16),
                pltpu.VMEM(levels.shape, bf16),
                pltpu.VMEM((1, CW), f32),
                pltpu.VMEM((4, CW), bf16),
                pltpu.VMEM((1, CW), f32),
                pltpu.SMEM((2,), i32),
                pltpu.SMEM((2,), i32),
                pltpu.VMEM((4, CW), bf16),
                pltpu.VMEM((4, CW), bf16),
                pltpu.VMEM((16, HEAD), f32),
                pltpu.VMEM((2, R // 2, CR, HEAD), bf16),
                pltpu.VMEM((R, CR, HEAD), bf16),
                pltpu.VMEM((R, CR, HEAD), bf16),
                pltpu.VMEM((2, 1, 128), i32),
                pltpu.VMEM((R, 1, 128), i32),
                pltpu.VMEM((2, 1, 128), i32),
                pltpu.SMEM((2, 1, 128), i32),
                pltpu.VMEM((T, 4 * CW // 128, 128), bf16),
                pltpu.VMEM((T, 4 * CW // 128, 128), bf16),
                pltpu.VMEM((4, 128), f32),
                pltpu.VMEM((T, 4, 128), f32),
                pltpu.SemaphoreType.DMA((13,)),
                pltpu.SemaphoreType.DMA((4,)),
                pltpu.SemaphoreType.DMA((2,)),
                pltpu.SemaphoreType.DMA((4,)),
                pltpu.SemaphoreType.DMA((2,)),
                pltpu.SemaphoreType.DMA((2,)),
                pltpu.SemaphoreType.DMA((5,)),
            ],
            compiler_params=pltpu.CompilerParams(
                collective_id=0, has_side_effects=True, vmem_limit_bytes=60 * 1024 * 1024
            ),
            name="decode_and_migrate",
        )(
            bt.T,
            cb,
            mreq,
            mdest,
            kpool,
            vpool,
            q,
            kn.reshape(4, HEAD),
            vn.reshape(4, HEAD),
            levels,
            scale[None, :],
            res,
            gain[None, :],
        )
        hid, norm, rk, rv, cnt, src = pl.pallas_call(
            functools.partial(emit, 6),
            out_shape=tuple(jax.ShapeDtypeStruct(r.shape, r.dtype) for r in results),
            in_specs=[hbm] * 6,
            out_specs=(hbm,) * 6,
            scratch_shapes=[pltpu.VMEM(r.shape, r.dtype) for r in results]
            + [pltpu.SemaphoreType.DMA((2, 6))],
            compiler_params=pltpu.CompilerParams(vmem_limit_bytes=60 * 1024 * 1024),
            name="write_outputs",
        )(*results)
        shape = (2, 2, 1, BLOCK, HEAD)
        return hid, norm, rk.reshape(shape), rv.reshape(shape), cnt, src

    return jax.shard_map(
        shards,
        mesh=mesh,
        in_specs=(
            P("replica", "tp", None),
            P("replica", "tp", None),
            P("replica", "tp", None),
            P("replica", "tp", None, None),
            P("replica", "tp", None, None),
            P("replica", None),
            P("replica"),
            P("replica"),
            P("replica"),
            P("tp", None),
            P("tp"),
            P("replica", "tp"),
            P("tp"),
        ),
        out_specs=(
            P("replica", "tp"),
            P("replica", "tp"),
            P("replica", None, "tp", None, None),
            P("replica", None, "tp", None, None),
            P("replica"),
            P("replica"),
        ),
        check_vma=False,
    )
```

```python
import functools
import math

import jax
import jax.numpy as jnp
from jax import lax
from jax.experimental import pallas as pl
from jax.experimental.pallas import tpu as pltpu
from jax.sharding import PartitionSpec as P

MESH = pl.DeviceIdType.MESH
BLOCK = 128
HEAD = 128
ROWS = 512


def outward(centre, i):
    return jnp.where(lax.rem(i, 2) == 1, centre - (i + 1) // 2, centre + i // 2)


def spread(n):
    return sorted(range(n), key=lambda d: -min(d, n - d))


def body(
    R,
    T,
    bt_hbm,
    cb_hbm,
    mreq_hbm,
    mdest_hbm,
    kpool_hbm,
    vpool_hbm,
    q_hbm,
    kn_hbm,
    vn_hbm,
    levels_hbm,
    scale_hbm,
    res_hbm,
    gain_hbm,
    hid_out,
    norm_out,
    rk_ref,
    rv_ref,
    cnt_out,
    src_out,
    bt,
    cb,
    mreq,
    mdest,
    kpool,
    vpool,
    q_ref,
    kn_ref,
    vn_ref,
    levels,
    scale_ref,
    res_ref,
    gain_ref,
    cnt_ref,
    src_ref,
    hid_ref,
    norm_ref,
    q16,
    stage,
    rx1,
    tx2,
    row,
    table,
    info,
    info_s,
    rs_tx,
    rs_rx,
    ss_tx,
    ss_rx,
    in_sem,
    mig_sem,
    meta_sem,
    info_sem,
    rs_sem,
    ss_sem,
    out_sem,
):
    me = lax.axis_index("replica")
    tp = lax.axis_index("tp")
    CR = 2 * ROWS // R
    per_block = BLOCK // CR
    half = R // 2
    Z = min(8, R // 2)
    Y = R // (2 * Z)
    my_y, my_z, core = me // (2 * Z), lax.rem(me // 2, Z), lax.rem(me, 2)

    ys = [lax.rem(my_y + d, Y) for d in spread(Y)]

    def plane(z):
        chips = [(y * Z + z) * 2 for y in ys]
        return [chip + c for chip in chips for c in (1 - core, core)]

    def farthest_first(i):
        return lax.rem(my_z + outward(Z // 2, i), Z)

    copies = [
        pltpu.make_async_copy(src, dst, in_sem.at[n])
        for n, (src, dst) in enumerate(
            (
                (bt_hbm, bt),
                (cb_hbm, cb),
                (mreq_hbm, mreq),
                (mdest_hbm, mdest),
                (kpool_hbm, kpool),
                (vpool_hbm, vpool),
                (q_hbm, q_ref),
                (kn_hbm, kn_ref),
                (vn_hbm, vn_ref),
                (levels_hbm, levels),
                (scale_hbm, scale_ref),
                (res_hbm, res_ref),
                (gain_hbm, gain_ref),
            )
        )
    ]
    for c in copies[:6]:
        c.start()

    barrier = pltpu.get_barrier_semaphore()

    def greet(to):
        pl.semaphore_signal(barrier, inc=1, device_id={"replica": to}, device_id_type=MESH)

    @pl.loop(0, Z)
    def _(i):
        peers = plane(farthest_first(i))
        for to in peers[:-1]:
            greet(to)

        @pl.when(i < Z - 1)
        def _():
            greet(peers[-1])

    @pl.loop(1, T)
    def _(i):
        pl.semaphore_signal(
            barrier, inc=1, device_id={"tp": lax.rem(tp + i, T)}, device_id_type=MESH
        )

    for c in copies[6:]:
        c.start()
    for c in copies[:4]:
        c.wait()

    lane = lax.broadcasted_iota(jnp.int32, (1, 128), 1)
    r0, r1 = mreq[0], mreq[1]
    c0, c1 = cb[r0], cb[r1]
    for j, c in enumerate((c0, c1)):
        row[j] = jnp.where(lane == mdest[j], me, 0) + jnp.where(lane == 64 + mdest[j], c, 0)
    table[me] = row[core]
    copies[4].wait()
    copies[5].wait()
    for j, (r, c) in enumerate(((r0, c0), (r1, c1))):
        for kv, pool in enumerate((kpool, vpool)):
            for b in range(2):
                blk = pool[bt[b, r], 0]
                if b == 1:
                    blk = jnp.where(c > 1, blk, jnp.zeros_like(blk))
                at = (kv * 2 + b) * per_block
                stage[j, at : at + per_block] = blk.reshape(per_block, CR, HEAD)
    my_j = lax.rem(me, 2)
    my_t = me // 2
    rx1[me] = stage[my_j, my_t]

    CW = levels.shape[1] // T

    def compute():
        for c in copies[6:9]:
            c.wait()

        for h in range(4):
            for i in range(4):
                q16[4 * h + i : 4 * h + i + 1, :] = q_ref[i, h : h + 1, :].astype(jnp.float32)
        q = q16[...].astype(jnp.bfloat16)
        kn, vn = kn_ref[...], vn_ref[...]
        sm = 1.0 / math.sqrt(HEAD)
        keys = kpool[...].reshape(8 * BLOCK, HEAD)
        dims = (((1,), (1,)), ((), ()))
        scores = lax.dot_general(q, keys, dims, preferred_element_type=jnp.float32) * sm
        own4 = lax.dot_general(q, kn, dims, preferred_element_type=jnp.float32) * sm
        req = lax.rem(lax.broadcasted_iota(jnp.int32, (16, 1), 0), 4)
        first, second = jnp.full((16, 1), -1, jnp.int32), jnp.full((16, 1), -1, jnp.int32)
        for i in range(4):
            first = jnp.where(req == i, bt[0, i], first)
            second = jnp.where(req == i, jnp.where(cb[i] > 1, bt[1, i], -1), second)
        column = lax.broadcasted_iota(jnp.int32, (16, 8 * BLOCK), 1) // BLOCK
        live = (column == first) | (column == second)
        mine = lax.broadcasted_iota(jnp.int32, (16, 4), 1) == req
        own = jnp.sum(jnp.where(mine, own4, 0.0), axis=1, keepdims=True)
        masked = jnp.where(live, scores, jnp.float32(-1e30))
        top = jnp.maximum(jnp.max(masked, axis=1, keepdims=True), own)
        expo = jnp.where(live, jnp.exp(masked - top), 0.0)
        self_expo = jnp.exp(own - top)
        total = jnp.sum(expo, axis=1, keepdims=True) + self_expo
        weights = (expo / total).astype(jnp.bfloat16)
        self_weight = jnp.where(mine, self_expo / total, 0.0).astype(jnp.bfloat16)
        mixed = jnp.dot(
            weights, vpool[...].reshape(8 * BLOCK, HEAD), preferred_element_type=jnp.float32
        ) + jnp.dot(self_weight, vn, preferred_element_type=jnp.float32)
        attn = jnp.concatenate([mixed[4 * h : 4 * h + 4] for h in range(4)], axis=1).astype(
            jnp.bfloat16
        )

        copies[9].wait()

        @pl.loop(0, T)
        def _(to):
            part = jnp.dot(
                attn,
                levels[:, pl.ds(pl.multiple_of(to * CW, CW), CW)],
                preferred_element_type=jnp.float32,
            )
            piece = jnp.concatenate(
                [part[:, 128 * k : 128 * k + 128] for k in range(CW // 128)], axis=0
            )
            rs_tx[to] = piece.astype(jnp.bfloat16)

    hid_copy = pltpu.make_async_copy(hid_ref, hid_out, out_sem.at[2])

    def reduce_scatter():
        rs_rx[tp] = rs_tx[tp]

        @pl.loop(1, T)
        def _(i):
            to = lax.rem(tp + i, T)
            pltpu.make_async_remote_copy(
                src_ref=rs_tx.at[to],
                dst_ref=rs_rx.at[tp],
                send_sem=rs_sem.at[0],
                recv_sem=rs_sem.at[1],
                device_id={"tp": to},
                device_id_type=MESH,
            ).start()

    def finish_hidden():
        for c in copies[10:]:
            c.wait()

        pltpu.make_async_copy(
            rs_rx.at[pl.ds(0, T - 1)], rs_rx.at[pl.ds(0, T - 1)], rs_sem.at[1]
        ).wait()
        sixteen = jnp.sum(rs_rx[...].astype(jnp.float32), axis=0)
        summed = jnp.concatenate([sixteen[4 * k : 4 * k + 4] for k in range(CW // 128)], axis=1)
        hidden = (summed * scale_ref[...] + res_ref[...].astype(jnp.float32)).astype(jnp.bfloat16)
        hid_ref[...] = hidden
        hid_copy.start()
        wide = hidden.astype(jnp.float32)
        square = jnp.sum(wide * wide, axis=1, keepdims=True)
        ss_tx[...] = jnp.broadcast_to(square, (4, 128))
        ss_rx[tp] = ss_tx[...]

        @pl.loop(1, T)
        def _(i):
            pltpu.make_async_remote_copy(
                src_ref=ss_tx,
                dst_ref=ss_rx.at[tp],
                send_sem=ss_sem.at[0],
                recv_sem=ss_sem.at[1],
                device_id={"tp": lax.rem(tp + i, T)},
                device_id_type=MESH,
            ).start()

    early = my_z < Z // 2
    pl.when(early)(compute)

    pl.semaphore_wait(barrier, R + T - 2)

    pl.when(early)(reduce_scatter)

    def announce(to):
        pltpu.make_async_remote_copy(
            src_ref=row.at[lax.rem(to, 2)],
            dst_ref=table.at[me],
            send_sem=meta_sem.at[0],
            recv_sem=meta_sem.at[1],
            device_id={"replica": to},
            device_id_type=MESH,
        ).start()

    def scatter(to):
        pltpu.make_async_remote_copy(
            src_ref=stage.at[lax.rem(to, 2), to // 2],
            dst_ref=rx1.at[me],
            send_sem=mig_sem.at[0],
            recv_sem=mig_sem.at[1],
            device_id={"replica": to},
            device_id_type=MESH,
        ).start()

    @pl.loop(0, Z)
    def _(i):
        peers = plane(farthest_first(i))
        for to in peers[:-1]:
            announce(to)

        @pl.when(i < Z - 1)
        def _():
            announce(peers[-1])

    @pl.loop(0, Z)
    def _(i):
        z = Z - 1 - i
        peers = plane(z)
        for to in peers[:-1]:
            scatter(to)

        @pl.when(z != my_z)
        def _():
            scatter(peers[-1])

    @pl.when(jnp.logical_not(early))
    def _():
        compute()
        reduce_scatter()

    pl.when(early)(finish_hidden)

    pltpu.make_async_copy(
        table.at[pl.ds(0, R - 1)], table.at[pl.ds(0, R - 1)], meta_sem.at[1]
    ).wait()
    info[0] = jnp.minimum(jnp.sum(table[...], axis=0), R - 1)
    info_copy = pltpu.make_async_copy(info.at[0], info_s.at[0], info_sem.at[0])
    info_copy.start()
    swap = pltpu.make_async_remote_copy(
        src_ref=info.at[0],
        dst_ref=info.at[1],
        send_sem=info_sem.at[1],
        recv_sem=info_sem.at[2],
        device_id={"replica": me + 1 - 2 * core},
        device_id_type=MESH,
    )
    swap.start()

    info_copy.wait()
    pltpu.make_async_copy(
        rx1.at[pl.ds(0, R - 1)], rx1.at[pl.ds(0, R - 1)], mig_sem.at[1]
    ).wait()
    my_b = lax.rem(my_t // per_block, 2)
    my_k = lax.rem(my_t, per_block)

    def deliver(out):
        def send(to):
            pltpu.make_async_remote_copy(
                src_ref=tx2.at[to],
                dst_ref=out.at[my_j, my_b, 0, my_k],
                send_sem=mig_sem.at[2],
                recv_sem=mig_sem.at[3],
                device_id={"replica": to},
                device_id_type=MESH,
            ).start()

        @pl.loop(0, Z)
        def _(z):
            peers = plane(z)
            pieces = [rx1[info_s[0, 0, to]] for to in peers]
            for to, piece in zip(peers, pieces):
                tx2[to] = piece
            for to in peers[:-1]:
                send(to)

            @pl.when(z != my_z)
            def _():
                send(peers[-1])

        pltpu.make_async_copy(tx2.at[me], out.at[my_j, my_b, 0, my_k], out_sem.at[4]).start()

    @pl.when(my_t < half // 2)
    def _():
        deliver(rk_ref)

    @pl.when(my_t >= half // 2)
    def _():
        deliver(rv_ref)

    swap.wait()
    swap_copy = pltpu.make_async_copy(info.at[1], info_s.at[1], info_sem.at[3])
    swap_copy.start()
    swap_copy.wait()
    for j in range(2):
        k = jnp.where(core == j, 0, 1)
        src_ref[j] = info_s[k, 0, me]
        cnt_ref[j] = info_s[k, 0, 64 + me]
    small = [
        pltpu.make_async_copy(cnt_ref, cnt_out, out_sem.at[0]),
        pltpu.make_async_copy(src_ref, src_out, out_sem.at[1]),
    ]
    for c in small:
        c.start()

    small.append(hid_copy)
    pl.when(jnp.logical_not(early))(finish_hidden)

    pltpu.make_async_copy(
        ss_rx.at[pl.ds(0, T - 1)], ss_rx.at[pl.ds(0, T - 1)], ss_sem.at[1]
    ).wait()
    wide = hid_ref[...].astype(jnp.float32)
    mean = jnp.sum(ss_rx[...], axis=0)[:, 0:1] / (CW * T)
    norm_ref[...] = (wide * lax.rsqrt(mean + 1e-5) * gain_ref[...]).astype(jnp.bfloat16)

    small.append(pltpu.make_async_copy(norm_ref, norm_out, out_sem.at[3]))
    small[-1].start()

    for c in small:
        c.wait()
    pltpu.make_async_copy(tx2.at[0], rk_ref.at[0, 0, 0, 0], out_sem.at[4]).wait()
    for buf, count, sem in (
        (rx1, R - 1, mig_sem.at[0]),
        (rx1, R - 1, mig_sem.at[2]),
        (rx1, R - 1, mig_sem.at[3]),
        (rs_tx, T - 1, rs_sem.at[0]),
        (ss_rx, T - 1, ss_sem.at[0]),
        (table, R - 1, meta_sem.at[0]),
    ):
        pltpu.make_async_copy(buf.at[pl.ds(0, count)], buf.at[pl.ds(0, count)], sem).wait()


def emit(n, *refs):
    ins, outs, held, sem = refs[:n], refs[n : 2 * n], refs[2 * n : 3 * n], refs[3 * n]
    loads = [pltpu.make_async_copy(ins[i], held[i], sem.at[0, i]) for i in range(n)]
    stores = [pltpu.make_async_copy(held[i], outs[i], sem.at[1, i]) for i in range(n)]
    for c in loads:
        c.start()
    for c, d in zip(loads, stores):
        c.wait()
        d.start()
    for c in stores:
        c.wait()


def solution(mesh):
    R, T = mesh.shape["replica"], mesh.shape["tp"]
    CR = 2 * ROWS // R
    per_block = BLOCK // CR

    def shards(q, kn, vn, kpool, vpool, bt, cb, mreq, mdest, levels, scale, res, gain):
        CW = levels.shape[1] // T
        vmem = pl.BlockSpec(memory_space=pltpu.VMEM)
        hbm = pl.BlockSpec(memory_space=pltpu.HBM)
        moved = (2, 2, 1, per_block, CR, HEAD)
        bf16, f32, i32 = jnp.bfloat16, jnp.float32, jnp.int32
        results = pl.pallas_call(
            functools.partial(body, R, T),
            out_shape=(
                jax.ShapeDtypeStruct((4, CW), bf16),
                jax.ShapeDtypeStruct((4, CW), bf16),
                jax.ShapeDtypeStruct(moved, bf16),
                jax.ShapeDtypeStruct(moved, bf16),
                jax.ShapeDtypeStruct((2,), i32),
                jax.ShapeDtypeStruct((2,), i32),
            ),
            in_specs=[hbm] * 13,
            out_specs=(hbm,) * 6,
            scratch_shapes=[
                pltpu.SMEM((2, 4), i32),
                pltpu.SMEM((4,), i32),
                pltpu.SMEM((2,), i32),
                pltpu.SMEM((2,), i32),
                pltpu.VMEM((8, 1, BLOCK, HEAD), bf16),
                pltpu.VMEM((8, 1, BLOCK, HEAD), bf16),
                pltpu.VMEM((4, 4, HEAD), bf16),
                pltpu.VMEM((4, HEAD), bf16),
                pltpu.VMEM((4, HEAD), bf16),
                pltpu.VMEM(levels.shape, bf16),
                pltpu.VMEM((1, CW), f32),
                pltpu.VMEM((4, CW), bf16),
                pltpu.VMEM((1, CW), f32),
                pltpu.SMEM((2,), i32),
                pltpu.SMEM((2,), i32),
                pltpu.VMEM((4, CW), bf16),
                pltpu.VMEM((4, CW), bf16),
                pltpu.VMEM((16, HEAD), f32),
                pltpu.VMEM((2, R // 2, CR, HEAD), bf16),
                pltpu.VMEM((R, CR, HEAD), bf16),
                pltpu.VMEM((R, CR, HEAD), bf16),
                pltpu.VMEM((2, 1, 128), i32),
                pltpu.VMEM((R, 1, 128), i32),
                pltpu.VMEM((2, 1, 128), i32),
                pltpu.SMEM((2, 1, 128), i32),
                pltpu.VMEM((T, 4 * CW // 128, 128), bf16),
                pltpu.VMEM((T, 4 * CW // 128, 128), bf16),
                pltpu.VMEM((4, 128), f32),
                pltpu.VMEM((T, 4, 128), f32),
                pltpu.SemaphoreType.DMA((13,)),
                pltpu.SemaphoreType.DMA((4,)),
                pltpu.SemaphoreType.DMA((2,)),
                pltpu.SemaphoreType.DMA((4,)),
                pltpu.SemaphoreType.DMA((2,)),
                pltpu.SemaphoreType.DMA((2,)),
                pltpu.SemaphoreType.DMA((5,)),
            ],
            compiler_params=pltpu.CompilerParams(
                collective_id=0, has_side_effects=True, vmem_limit_bytes=60 * 1024 * 1024
            ),
            name="decode_and_migrate",
        )(
            bt.T,
            cb,
            mreq,
            mdest,
            kpool,
            vpool,
            q,
            kn.reshape(4, HEAD),
            vn.reshape(4, HEAD),
            levels,
            scale[None, :],
            res,
            gain[None, :],
        )
        hid, norm, rk, rv, cnt, src = pl.pallas_call(
            functools.partial(emit, 6),
            out_shape=tuple(jax.ShapeDtypeStruct(r.shape, r.dtype) for r in results),
            in_specs=[hbm] * 6,
            out_specs=(hbm,) * 6,
            scratch_shapes=[pltpu.VMEM(r.shape, r.dtype) for r in results]
            + [pltpu.SemaphoreType.DMA((2, 6))],
            compiler_params=pltpu.CompilerParams(vmem_limit_bytes=60 * 1024 * 1024),
            name="write_outputs",
        )(*results)
        shape = (2, 2, 1, BLOCK, HEAD)
        return hid, norm, rk.reshape(shape), rv.reshape(shape), cnt, src

    return jax.shard_map(
        shards,
        mesh=mesh,
        in_specs=(
            P("replica", "tp", None),
            P("replica", "tp", None),
            P("replica", "tp", None),
            P("replica", "tp", None, None),
            P("replica", "tp", None, None),
            P("replica", None),
            P("replica"),
            P("replica"),
            P("replica"),
            P("tp", None),
            P("tp"),
            P("replica", "tp"),
            P("tp"),
        ),
        out_specs=(
            P("replica", "tp"),
            P("replica", "tp"),
            P("replica", None, "tp", None, None),
            P("replica", None, "tp", None, None),
            P("replica"),
            P("replica"),
        ),
        check_vma=False,
    )
```
